32 devices in a mesh: grp: 2 (over x), slc: 16 (over z, y, core).
Axes of the slice: x: 2, y: 2, z: 4, core: 2. Of those that a mesh axis runs over, the one named last changes fastest.
Arguments:
- potential: float32 [32, 512, 512], P(('grp', 'slc')), parts along dimension 0, may hold values from -6 to 6
- thickness: int32 [32], P(('grp', 'slc')), parts along dimension 0, may hold values from 1 to 3
- propagator_phase: float32 [128], replicated, may hold values from -3.140625 to 3.140625
- probe: bfloat16 [4, 12, 128, 128], P('grp'), parts along dimension 0, may hold values from -1.1953125 to 1.1953125
- offsets: int32 [2, 2], P('grp'), parts along dimension 0, may hold values from 0 to 384
- measured: float32 [2, 128, 128], P('grp'), parts along dimension 0, may hold values from 0 to 2
Outputs:
- gradient: float32 [32, 512, 512], P(('grp', 'slc')), parts along dimension 0
The draws below stay inside these ranges and needn't reach their ends.
There are 2 independent parts, one for each index of `grp`. The reference program is written for one: setup_inputs(seed, part) draws one part's arguments, and reference() takes and returns one part's arrays. A program takes and returns all parts, laid end to end along the dimension named above; an argument that names none is the same for every part. Nothing has to cross between parts.
Inputs may be any that keep to these rules, and one draw needn't show every extreme that they name: `thickness`: slice thicknesses are whole numbers of base steps. `offsets`: each panel lies inside the object field.
All inputs are finite; a program needn't handle non-finite values.
Results may differ from the reference program's by a relative error of at most 0.0003.
Values sent between devices are 32-bit elements; how exact they have to be, the bound alone decides.
No kernel may reach another device: no remote copies, remote signals or barrier semaphores. Data moves between devices by JAX's collectives and lax.ppermute only.
A program may use at most 64 MiB of HBM per device.

```python
import math
import jax
import jax.numpy as jnp
from jax import lax

PANEL = 128
MODES = 12
POS = 1
OBJ = 512
NSLICES = 16


def with_ends(result, stream_key, low, largest):
    longest = result.shape.index(max(result.shape))
    spots = []
    for shift in (0, 1):
        where = [jax.random.randint(jax.random.fold_in(stream_key, axis), (), 0, length) for axis, length in enumerate(result.shape)]
        where[longest] = (where[longest] + shift) % result.shape[longest]
        spots.append(tuple(where))
    return result.at[spots[0]].set(low).at[spots[1]].set(largest)


def levels(key, extent, pieces, least, top_value):
    def one(dim, shards_of):
        heights = jax.random.uniform(jax.random.fold_in(jax.random.fold_in(key, 6), dim), (shards_of,), jnp.float32, least / len(pieces), top_value / len(pieces))
        return jnp.repeat(jnp.exp(heights), extent[dim] // shards_of).reshape((-1,) + (1,) * (len(extent) - dim - 1))

    loudness = one(*pieces[0])
    for cut in pieces[1:]:
        loudness = loudness * one(*cut)
    return loudness


def centred(key, extent, spread, reach, cuts=(), kind=jnp.bfloat16):
    gain = levels(key, extent, cuts, -0.22, 0.18) if cuts else 1.0
    array = jax.random.normal(key, extent, jnp.float32) * spread * gain
    return jnp.minimum(jnp.maximum(array, -reach), reach).astype(kind)


def setup_inputs(seed: int = 0, part: int = 0) -> dict:
    key_of = jax.random.split(jax.random.key(seed), 7)
    part_splits = jax.random.split(jax.random.fold_in(key_of[6], part), 7)
    potential = centred(part_splits[0], (NSLICES, OBJ, OBJ), 1.0, 6.0, ((0, 16),), jnp.float32)
    thickness = with_ends(jax.random.randint(part_splits[1], (NSLICES,), 1, 4), jax.random.fold_in(part_splits[1], 1), 1, 3).astype(jnp.int32)
    propagator_phase = jnp.clip(jax.random.uniform(key_of[2], (PANEL,), jnp.float32, -3.140625, 3.140625), -3.140625, 3.140625)
    probe = centred(part_splits[3], (2, MODES, PANEL, PANEL), 0.2, 1.1953125)
    offsets = jax.random.randint(part_splits[4], (POS, 2), 0, OBJ - PANEL + 1).astype(jnp.int32)
    measured = jnp.clip(jax.random.uniform(part_splits[5], (POS, PANEL, PANEL), jnp.float32, 0.0, 2.0), 0.0, 2.0)
    return {"potential": potential, "thickness": thickness, "propagator_phase": propagator_phase, "probe": probe, "offsets": offsets, "measured": measured}


HIGH = lax.Precision.HIGHEST

def dft_tables(table_size):
    indices = jnp.arange(table_size, dtype=jnp.int32)
    products = indices[:, None] * indices[None, :] % table_size
    angle_grid = products.astype(jnp.float32) * (2.0 * math.pi / table_size)
    return (jnp.cos(angle_grid), jnp.sin(angle_grid))

def propagator(phase_table, thickness_value, cos_grid, sin_grid):
    table_size = phase_table.shape[0]
    argument = thickness_value.astype(jnp.float32) * phase_table
    filter_real = jnp.cos(argument)
    filter_imag = jnp.sin(argument)
    mixed_real = cos_grid * filter_real[None, :] - sin_grid * filter_imag[None, :]
    mixed_imag = cos_grid * filter_imag[None, :] + sin_grid * filter_real[None, :]
    kernel_real = (jnp.dot(mixed_real, cos_grid, precision=HIGH) + jnp.dot(mixed_imag, sin_grid, precision=HIGH)) / table_size
    kernel_imag = (jnp.dot(mixed_imag, cos_grid, precision=HIGH) - jnp.dot(mixed_real, sin_grid, precision=HIGH)) / table_size
    return (kernel_real, kernel_imag)

def product(pattern, left_operand, right_operand):
    return jnp.einsum(pattern, left_operand.astype(jnp.float32), right_operand.astype(jnp.float32), precision=HIGH)

def left_apply(pattern, matrix_real, matrix_imag, current):
    real_part = product(pattern, matrix_real, current[0]) - product(pattern, matrix_imag, current[1])
    imag_part = product(pattern, matrix_real, current[1]) + product(pattern, matrix_imag, current[0])
    return jnp.stack([real_part, imag_part])

def right_apply(pattern, current, matrix_real, matrix_imag):
    real_part = product(pattern, current[0], matrix_real) - product(pattern, current[1], matrix_imag)
    imag_part = product(pattern, current[1], matrix_real) + product(pattern, current[0], matrix_imag)
    return jnp.stack([real_part, imag_part])

def propagate(kernel, current):
    half_way = left_apply('ab,mbc->mac', kernel[0], kernel[1], current)
    return right_apply('mab,cb->mac', half_way, kernel[0], kernel[1])

def back_propagate(kernel, current):
    half_way = left_apply('ba,mbc->mac', kernel[0], -kernel[1], current)
    return right_apply('mab,bc->mac', half_way, kernel[0], -kernel[1])

def transmit(patch, current):
    cosine = jnp.cos(patch)
    sine_part = jnp.sin(patch)
    real_part = cosine * current[0] - sine_part * current[1]
    imag_part = cosine * current[1] + sine_part * current[0]
    return jnp.stack([real_part, imag_part])

def untransmit(patch, pulled):
    cosine = jnp.cos(patch)
    sine_part = jnp.sin(patch)
    real_part = cosine * pulled[0] + sine_part * pulled[1]
    imag_part = cosine * pulled[1] - sine_part * pulled[0]
    return jnp.stack([real_part, imag_part])

def sensitivity(pulled, transmitted):
    return lax.optimization_barrier(jnp.sum(pulled[1] * transmitted[0] - pulled[0] * transmitted[1], axis=0))

def detector(exit_wave, panel_data, fourier):
    half_way = left_apply('ab,mbc->mac', fourier[0], fourier[1], exit_wave)
    far_field = right_apply('mab,cb->mac', half_way, fourier[0], fourier[1])
    intensity = lax.optimization_barrier(jnp.sum(far_field[0] * far_field[0] + far_field[1] * far_field[1], axis=0))
    misfit = intensity - panel_data
    weighted = far_field * misfit[None, None]
    half_back = left_apply('ba,mbc->mac', fourier[0], -fourier[1], weighted)
    return right_apply('mab,bc->mac', half_back, fourier[0], -fourier[1])

def reference(potential, thickness, propagator_phase, probe, offsets, measured):
    local_slices = potential.shape[0]
    panel_size = probe.shape[2]
    cos_grid, sin_grid = dft_tables(panel_size)
    norm_scale = 1.0 / math.sqrt(panel_size)
    fourier = (cos_grid * norm_scale, -sin_grid * norm_scale)
    kernels = lax.map(lambda thickness_value: propagator(propagator_phase, thickness_value, cos_grid, sin_grid), thickness)
    anchor = jnp.zeros((), jnp.int32)
    probe_wave = probe.astype(jnp.float32)

    def one_position(gradient, inputs):
        corner, panel_data = inputs
        row_start = corner[0].astype(jnp.int32)
        col_start = corner[1].astype(jnp.int32)
        patches = lax.dynamic_slice(potential, (anchor, row_start, col_start), (local_slices, panel_size, panel_size))

        def forward_step(current, inputs_slice):
            patch, kernel_real, kernel_imag = inputs_slice
            return (propagate((kernel_real, kernel_imag), transmit(patch, current)), current)
        exit_wave, stored = lax.scan(forward_step, probe_wave, (patches, kernels[0], kernels[1]))
        adjoint = detector(exit_wave, panel_data, fourier)

        def backward_step(current, inputs_slice):
            patch, kernel_real, kernel_imag, stored_wave = inputs_slice
            transmitted = transmit(patch, stored_wave)
            pulled = back_propagate((kernel_real, kernel_imag), current)
            return (untransmit(patch, pulled), sensitivity(pulled, transmitted))
        _, updates = lax.scan(backward_step, adjoint, (patches, kernels[0], kernels[1], stored), reverse=True)
        window = lax.dynamic_slice(gradient, (anchor, row_start, col_start), (local_slices, panel_size, panel_size))
        gradient = lax.dynamic_update_slice(gradient, window + updates, (anchor, row_start, col_start))
        return (gradient, None)
    gradient = jnp.zeros(potential.shape, jnp.float32)
    gradient, _ = lax.scan(one_position, gradient, (offsets, measured))
    return gradient
```

```python
import functools
import math

import jax
import jax.numpy as jnp
from jax import lax
from jax.experimental import pallas as pl
from jax.experimental.pallas import tpu as pltpu
from jax.sharding import PartitionSpec as P

F32 = jnp.float32
BF16 = jnp.bfloat16
CLUSTER = 4
LIMIT = 24 * 2**20
VMEM = pl.BlockSpec(memory_space=pltpu.VMEM)
SMEM = pl.BlockSpec(memory_space=pltpu.SMEM)
ANY = pl.BlockSpec(memory_space=pl.ANY)


def sincos(x):
    turns = jnp.floor(x * (2.0 / math.pi) + 0.5)
    r = x - turns * 1.5703125
    r = r - turns * 4.837512969970703125e-4
    r = r - turns * 7.549789948768648e-8
    r2 = r * r
    s = r + r * r2 * (-1.6666654611e-1 + r2 * (8.3321608736e-3 + r2 * -1.9515295891e-4))
    c = 1.0 - 0.5 * r2 + r2 * r2 * (
        4.166664568298827e-2 + r2 * (-1.388731625493765e-3 + r2 * 2.443315711809948e-5)
    )
    quadrant = turns.astype(jnp.int32)
    odd = (quadrant & 1) == 1
    sine = jnp.where(odd, c, s)
    cosine = jnp.where(odd, s, c)
    sine = jnp.where((quadrant & 2) == 2, -sine, sine)
    cosine = jnp.where(((quadrant + 1) & 2) == 2, -cosine, cosine)
    return cosine, sine


def split(x):
    high = x.astype(BF16)
    return high, (x - high.astype(F32)).astype(BF16)


def dot(a, b):
    return jnp.dot(a, b, preferred_element_type=F32)


def product(x, high, low):
    x_high, x_low = split(x)
    return dot(x_high, high) + dot(x_low, high) + dot(x_high, low)


def turned(x, size):
    return jnp.concatenate([x[:, :size].T, x[:, size:].T], axis=1)


def two_sided(x, high, low, size):
    return product(turned(product(x, high, low), size), high, low)


def window_of(offsets_ref, rows, columns, size):
    row, column = offsets_ref[0, 0], offsets_ref[0, 1]
    row_base = jnp.minimum(row // 8 * 8, rows - size - 8)
    column_base = jnp.minimum(column // 128 * 128, columns - 2 * size)
    return (
        pl.multiple_of(row_base, 8),
        pl.multiple_of(column_base, 128),
        row - row_base,
        column - column_base,
    )


def extract_kernel(offsets_ref, thickness_ref, potential_ref, out_ref, window, sem):
    size = out_ref.shape[1]
    row_base, column_base, down, across = window_of(
        offsets_ref, potential_ref.shape[1], potential_ref.shape[2], size
    )
    copy = pltpu.make_async_copy(
        potential_ref.at[0, pl.ds(row_base, size + 8), pl.ds(column_base, 2 * size)], window, sem
    )
    copy.start()
    out_ref[size:, :] = jnp.full((8, size), thickness_ref[0].astype(F32))
    copy.wait()
    part = pltpu.roll(window[...], lax.rem(size + 8 - down, size + 8), 0)[:size]
    shift = lax.rem(size - across, size)
    left = pltpu.roll(part[:, :size], shift, 1)
    right = pltpu.roll(part[:, size:], shift, 1)
    lane = lax.broadcasted_iota(jnp.int32, (size, size), 1)
    out_ref[:size, :] = jnp.where(lane < size - across, left, right)


def place_kernel(layer_ref, offsets_ref, own_ref, relayed_ref, other_ref, zeros_ref, out_ref, window, sem):
    del zeros_ref
    size = own_ref.shape[1]
    row_base, column_base, down, across = window_of(
        offsets_ref, out_ref.shape[1], out_ref.shape[2], size
    )
    first = jnp.where(layer_ref[0] == 0, own_ref[...], relayed_ref[...])
    update = jnp.concatenate([first + other_ref[...], jnp.zeros((8, size), F32)], axis=0)
    update = pltpu.roll(pltpu.roll(update, down, 0), lax.rem(across, size), 1)
    lane = lax.broadcasted_iota(jnp.int32, (size + 8, size), 1)
    window[:, :size] = jnp.where(lane < across, 0.0, update)
    window[:, size:] = jnp.where(lane < across, update, 0.0)
    copy = pltpu.make_async_copy(
        window, out_ref.at[0, pl.ds(row_base, size + 8), pl.ds(column_base, 2 * size)], sem
    )
    copy.start()
    copy.wait()


def table_kernel(phase_ref, forward_ref, backward_ref):
    size = phase_ref.shape[1]
    rows = lax.broadcasted_iota(jnp.int32, (size, size), 0)
    columns = lax.broadcasted_iota(jnp.int32, (size, size), 1)
    angle = ((rows * columns) % size).astype(F32) * (2.0 * math.pi / size)
    c, s = sincos(angle)
    whole = jnp.concatenate(
        [jnp.concatenate([c, s], axis=1), jnp.concatenate([-s, c], axis=1)], axis=0
    )

    def put(index, real, imag):
        real_turned, imag_turned = real.T, imag.T
        for ref, quarters in (
            (forward_ref, (real, imag, -imag, real)),
            (backward_ref, (real_turned, -imag_turned, imag_turned, real_turned)),
        ):
            for place, quarter in enumerate(quarters):
                r, k = place // 2 * size, place % 2 * size
                high, low = split(quarter)
                ref[index, 0, r : r + size, k : k + size] = high
                ref[index, 1, r : r + size, k : k + size] = low

    for steps in (1, 2, 3):
        h_real, h_imag = sincos(phase_ref[...] * float(steps))
        real = c * h_real + s * h_imag
        imag = c * h_imag - s * h_real
        put(2 + steps, real * (1.0 / math.sqrt(size)), imag * (1.0 / math.sqrt(size)))
        both = jnp.concatenate([real, imag], axis=1)
        k = jnp.dot(both, whole, precision=lax.Precision.HIGHEST, preferred_element_type=F32)
        put(steps - 1, k[:, :size] * (1.0 / size), k[:, size:] * (1.0 / size))


def steps_of(ref, index, size):
    steps = ref[index, size, 0].astype(jnp.int32)
    return jnp.clip(steps, 1, 3) - 1


def forward_kernel(last, place_ref, near_ref, far_ref, table_ref, wave_ref, *refs):
    if last:
        out_ref, sum_ref, stored_ref, cs_ref, patch = refs
    else:
        out_ref, stored_ref, cs_ref, patch = refs
    size = near_ref.shape[2]
    place = place_ref[0]
    patch[0] = near_ref[0]
    patch[2] = near_ref[1]
    patch[1] = far_ref[0]
    patch[3] = far_ref[1]
    modes = out_ref.shape[0]
    waves = [
        wave_ref[m]
        if wave_ref.dtype == F32
        else jnp.concatenate([wave_ref[0, m].astype(F32), wave_ref[1, m].astype(F32)], axis=1)
        for m in range(modes)
    ]
    for index in range(CLUSTER):
        at = index ^ place
        kind = steps_of(patch, at, size)
        if last and index == CLUSTER - 1:
            kind = kind + 3
        cosine, sine = sincos(patch[at, :size, :])
        if index % 2 == 1:
            cosine, sine = cosine.T, sine.T
        cs_ref[index, 0] = cosine
        cs_ref[index, 1] = sine
        slot = jnp.where(index // 2 == place // 2, (index ^ place) & 1, 2)
        high, low = table_ref[kind, 0], table_ref[kind, 1]
        after = []
        for m in range(modes):
            real, imag = waves[m][:, :size], waves[m][:, size:]
            u = jnp.concatenate([cosine * real - sine * imag, cosine * imag + sine * real], axis=1)
            stored_ref[slot, m] = u
            after.append(two_sided(u, high, low, size))
        waves = after
    total = None
    for m in range(modes):
        out_ref[m] = waves[m]
        if last:
            real, imag = waves[m][:, :size], waves[m][:, size:]
            power = real * real + imag * imag
            total = power if total is None else total + power
    if last:
        sum_ref[...] = total


def backward_kernel(last, place_ref, near_ref, far_ref, table_ref, stored_ref, cs_ref, wave_ref, *refs):
    if last:
        mine_ref, theirs_ref, measured_ref, out_ref, own_ref, other_ref, patch, update = refs
    else:
        out_ref, own_ref, other_ref, patch, update = refs
    size = near_ref.shape[2]
    place = place_ref[0]
    patch[0] = near_ref[0, size:, :]
    patch[2] = near_ref[1, size:, :]
    patch[1] = far_ref[0, size:, :]
    patch[3] = far_ref[1, size:, :]
    modes = out_ref.shape[0]
    waves = [wave_ref[m] for m in range(modes)]
    if last:
        misfit = mine_ref[...] + theirs_ref[...] - measured_ref[0]
        misfit = jnp.concatenate([misfit, misfit], axis=1)
        waves = [wave * misfit for wave in waves]
    for index in reversed(range(CLUSTER)):
        at = index ^ place
        kind = steps_of(patch, at, 0)
        if last and index == CLUSTER - 1:
            kind = kind + 3
        cosine, sine = cs_ref[index, 0], cs_ref[index, 1]
        slot = jnp.where(index // 2 == place // 2, (index ^ place) & 1, 2)
        high, low = table_ref[kind, 0], table_ref[kind, 1]
        after = []
        gradient = None
        for m in range(modes):
            mu = two_sided(waves[m], high, low, size)
            real, imag = mu[:, :size], mu[:, size:]
            u = stored_ref[slot, m]
            term = imag * u[:, :size] - real * u[:, size:]
            gradient = term if gradient is None else gradient + term
            after.append(
                jnp.concatenate([cosine * real + sine * imag, cosine * imag - sine * real], axis=1)
            )
        update[slot] = gradient.T if index % 2 == 1 else gradient
        waves = after
    for m in range(modes):
        out_ref[m] = waves[m]
    own_ref[...] = update[0]
    other_ref[...] = update[1]


def shaped(*shape, dtype=F32):
    return jax.ShapeDtypeStruct(shape, dtype)


def call(kernel, ins, outs, scratch=(), flops=0, **more):
    return pl.pallas_call(
        kernel,
        in_specs=ins,
        out_specs=[VMEM] * len(outs),
        out_shape=outs,
        scratch_shapes=list(scratch),
        compiler_params=pltpu.CompilerParams(vmem_limit_bytes=LIMIT),
        cost_estimate=pl.CostEstimate(flops=flops, bytes_accessed=2**20, transcendentals=0),
        **more,
    )


def local(potential, thickness, propagator_phase, probe, offsets, measured):
    size = probe.shape[2]
    modes = probe.shape[1] // 2
    length = lax.axis_size("slc")
    chunks = length // CLUSTER
    rank = lax.axis_index("slc")
    place = (rank % CLUSTER).reshape(1).astype(jnp.int32)
    layer = (rank // CLUSTER).reshape(1).astype(jnp.int32)
    wave = shaped(modes, size, 2 * size)

    def flipped(block, bit):
        return lax.ppermute(block, "slc", [(i, i ^ bit) for i in range(length)])

    def moved(block, layers):
        route = [(i, (i + CLUSTER * layers) % length) for i in range(length)]
        return lax.ppermute(block, "slc", route)

    message = pl.pallas_call(
        extract_kernel,
        in_specs=[SMEM, SMEM, ANY],
        out_specs=VMEM,
        out_shape=shaped(size + 8, size),
        scratch_shapes=[pltpu.VMEM((size + 8, 2 * size), F32), pltpu.SemaphoreType.DMA],
    )(offsets, thickness, potential)
    near = jnp.stack([message, flipped(message, 2)])
    forward_table, backward_table = call(
        table_kernel, [VMEM], [shaped(6, 2, 2 * size, 2 * size, dtype=BF16)] * 2, flops=10**9
    )(propagator_phase.reshape(1, size))
    waves = lax.dynamic_slice_in_dim(probe, (rank % 2) * modes, modes, 1)

    work = CLUSTER * modes * 2 * 3 * 2 * size * (2 * size) ** 2
    nears, fars, kept, tables = [], [], [], []
    power = None
    for chunk in range(chunks):
        last = chunk == chunks - 1
        if chunk > 0:
            near = moved(near, -1)
        far = flipped(near, 1)
        nears.append(near)
        fars.append(far)
        outs = [wave] + ([shaped(size, size)] if last else [])
        outs += [shaped(3, modes, size, 2 * size), shaped(CLUSTER, 2, size, size)]
        results = call(
            functools.partial(forward_kernel, last),
            [SMEM] + [VMEM] * 4,
            outs,
            [pltpu.VMEM((CLUSTER, size + 8, size), F32)],
            work,
        )(place, near, far, forward_table, waves)
        waves = results[0]
        if last:
            power = results[1]
        kept.append(results[-2:])
    extra = (power, flipped(power, 1), measured)
    travelling = None
    for chunk in reversed(range(chunks)):
        last = chunk == chunks - 1
        waves, own, other = call(
            functools.partial(backward_kernel, last),
            [SMEM] + [VMEM] * (9 if last else 6),
            [wave, shaped(size, size), shaped(size, size)],
            [pltpu.VMEM((CLUSTER, 8, size), F32), pltpu.VMEM((3, size, size), F32)],
            work,
        )(place, nears[chunk], fars[chunk], backward_table, *kept[chunk], waves, *(extra if last else ()))
        if chunk > 0:
            fresh = jnp.stack([own, other])
            if travelling is not None:
                fresh = jnp.where(layer[0] == 0, fresh, travelling)
            travelling = moved(fresh, 1)
    if travelling is None:
        travelling = jnp.stack([own, other])
    other = jnp.where(layer[0] == 0, other, travelling[1])
    other = flipped(other, 1)
    return pl.pallas_call(
        place_kernel,
        in_specs=[SMEM, SMEM, VMEM, VMEM, VMEM, ANY],
        out_specs=ANY,
        out_shape=shaped(*potential.shape),
        scratch_shapes=[pltpu.VMEM((size + 8, 2 * size), F32), pltpu.SemaphoreType.DMA],
        input_output_aliases={5: 0},
    )(layer, offsets, own, travelling[0], other, jnp.zeros(potential.shape, F32))


def solution(mesh):
    placed = (
        P(("grp", "slc"), None, None),
        P(("grp", "slc")),
        P(),
        P("grp", None, None, None),
        P("grp", None),
        P("grp", None, None),
    )
    return jax.shard_map(
        local, mesh=mesh, in_specs=placed, out_specs=P(("grp", "slc"), None, None), check_vma=False
    )
```

```python
import functools
import math

import jax
import jax.numpy as jnp
from jax import lax
from jax.experimental import pallas as pl
from jax.experimental.pallas import tpu as pltpu
from jax.sharding import PartitionSpec as P

F32 = jnp.float32
BF16 = jnp.bfloat16
CLUSTER = 4
LIMIT = 12 * 2**20
VMEM = pl.BlockSpec(memory_space=pltpu.VMEM)
SMEM = pl.BlockSpec(memory_space=pltpu.SMEM)
HBM = pl.BlockSpec(memory_space=pltpu.HBM)
ANY = pl.BlockSpec(memory_space=pl.ANY)


def sincos(x):
    turns = jnp.floor(x * (2.0 / math.pi) + 0.5)
    r = x - turns * 1.5703125
    r = r - turns * 4.837512969970703125e-4
    r = r - turns * 7.549789948768648e-8
    r2 = r * r
    s = r + r * r2 * (-1.6666654611e-1 + r2 * (8.3321608736e-3 + r2 * -1.9515295891e-4))
    c = 1.0 - 0.5 * r2 + r2 * r2 * (
        4.166664568298827e-2 + r2 * (-1.388731625493765e-3 + r2 * 2.443315711809948e-5)
    )
    quadrant = turns.astype(jnp.int32)
    odd = (quadrant & 1) == 1
    sine = jnp.where(odd, c, s)
    cosine = jnp.where(odd, s, c)
    sine = jnp.where((quadrant & 2) == 2, -sine, sine)
    cosine = jnp.where(((quadrant + 1) & 2) == 2, -cosine, cosine)
    return cosine, sine


def split(x):
    high = x.astype(BF16)
    return high, (x - high.astype(F32)).astype(BF16)


def dot(a, b):
    return jnp.dot(a, b, preferred_element_type=F32)


def product(x, high, low):
    x_high, x_low = split(x)
    return dot(x_high, high) + dot(x_low, high) + dot(x_high, low)


def turned(x, size):
    return jnp.concatenate([x[:, :size].T, x[:, size:].T], axis=1)


def two_sided(x, high, low, size):
    return product(turned(product(x, high, low), size), high, low)


def window_of(offsets_ref, rows, columns, size):
    row, column = offsets_ref[0, 0], offsets_ref[0, 1]
    row_base = jnp.minimum(row // 8 * 8, rows - size - 8)
    column_base = jnp.minimum(column // 128 * 128, columns - 2 * size)
    return (
        pl.multiple_of(row_base, 8),
        pl.multiple_of(column_base, 128),
        row - row_base,
        column - column_base,
    )


def extract_kernel(offsets_hbm, thickness_hbm, potential_ref, out_ref, window, offsets_ref, thickness_ref, sems):
    size = out_ref.shape[1]
    corner = pltpu.make_async_copy(offsets_hbm, offsets_ref, sems.at[0])
    steps = pltpu.make_async_copy(thickness_hbm, thickness_ref, sems.at[1])
    corner.start()
    steps.start()
    corner.wait()
    row_base, column_base, down, across = window_of(
        offsets_ref, potential_ref.shape[1], potential_ref.shape[2], size
    )
    copy = pltpu.make_async_copy(
        potential_ref.at[0, pl.ds(row_base, size + 8), pl.ds(column_base, 2 * size)], window, sems.at[2]
    )
    copy.start()
    steps.wait()
    out_ref[size:, :] = jnp.full((8, size), thickness_ref[0].astype(F32))
    copy.wait()
    part = pltpu.roll(window[...], lax.rem(size + 8 - down, size + 8), 0)[:size]
    shift = lax.rem(size - across, size)
    left = pltpu.roll(part[:, :size], shift, 1)
    right = pltpu.roll(part[:, size:], shift, 1)
    lane = lax.broadcasted_iota(jnp.int32, (size, size), 1)
    out_ref[:size, :] = jnp.where(lane < size - across, left, right)


def place_kernel(offsets_ref, ours_ref, theirs_ref, zeros_ref, out_ref, window, sem):
    del zeros_ref
    size = theirs_ref.shape[1]
    row_base, column_base, down, across = window_of(
        offsets_ref, out_ref.shape[1], out_ref.shape[2], size
    )
    update = jnp.concatenate([ours_ref[...] + theirs_ref[...], jnp.zeros((8, size), F32)], axis=0)
    update = pltpu.roll(pltpu.roll(update, down, 0), lax.rem(across, size), 1)
    lane = lax.broadcasted_iota(jnp.int32, (size + 8, size), 1)
    window[:, :size] = jnp.where(lane < across, 0.0, update)
    window[:, size:] = jnp.where(lane < across, update, 0.0)
    copy = pltpu.make_async_copy(
        window, out_ref.at[0, pl.ds(row_base, size + 8), pl.ds(column_base, 2 * size)], sem
    )
    copy.start()
    copy.wait()


def table_kernel(phase_ref, forward_ref, backward_ref, zeros_ref, blank, sem):
    size = phase_ref.shape[1]
    blank[...] = jnp.zeros_like(blank)
    copies = [
        pltpu.make_async_copy(blank, zeros_ref.at[0, pl.ds(row, size)], sem.at[k])
        for k, row in enumerate(range(0, zeros_ref.shape[1], size))
    ]
    for copy in copies:
        copy.start()
    rows = lax.broadcasted_iota(jnp.int32, (size, size), 0)
    columns = lax.broadcasted_iota(jnp.int32, (size, size), 1)
    angle = ((rows * columns) % size).astype(F32) * (2.0 * math.pi / size)
    c, s = sincos(angle)
    whole = jnp.concatenate(
        [jnp.concatenate([c, s], axis=1), jnp.concatenate([-s, c], axis=1)], axis=0
    )

    def put(index, real, imag):
        real_turned, imag_turned = real.T, imag.T
        for ref, quarters in (
            (forward_ref, (real, imag, -imag, real)),
            (backward_ref, (real_turned, -imag_turned, imag_turned, real_turned)),
        ):
            for place, quarter in enumerate(quarters):
                r, k = place // 2 * size, place % 2 * size
                high, low = split(quarter)
                ref[index, 0, r : r + size, k : k + size] = high
                ref[index, 1, r : r + size, k : k + size] = low

    for steps in (1, 2, 3):
        h_real, h_imag = sincos(phase_ref[...] * float(steps))
        real = c * h_real + s * h_imag
        imag = c * h_imag - s * h_real
        put(2 + steps, real * (1.0 / math.sqrt(size)), imag * (1.0 / math.sqrt(size)))
        both = jnp.concatenate([real, imag], axis=1)
        k = jnp.dot(both, whole, precision=lax.Precision.HIGHEST, preferred_element_type=F32)
        put(steps - 1, k[:, :size] * (1.0 / size), k[:, size:] * (1.0 / size))
    for copy in copies:
        copy.wait()


def steps_of(ref, index, size):
    steps = ref[index, size, 0].astype(jnp.int32)
    return jnp.clip(steps, 1, 3) - 1


def position():
    rank = lax.axis_index("slc")
    return rank, rank // CLUSTER


def patch_of(near_ref, far_ref, at, size):
    block, half, crossed = at // CLUSTER, (at // 2) % 2, at % 2 == 1
    entry = 2 * block + half
    steps = jnp.where(crossed, far_ref[entry, size, 0], near_ref[entry, size, 0])
    kind = jnp.clip(steps.astype(jnp.int32), 1, 3) - 1
    cosine, sine = sincos(jnp.where(crossed, far_ref[entry, :size, :], near_ref[entry, :size, :]))
    return kind, cosine, sine


def first_waves(wave_ref, modes):
    if wave_ref.dtype == F32:
        return [wave_ref[m] for m in range(modes)]
    start = (lax.axis_index("slc") % 2) * modes
    return [
        jnp.concatenate(
            [wave_ref[0, start + m].astype(F32), wave_ref[1, start + m].astype(F32)], axis=1
        )
        for m in range(modes)
    ]


def forward_kernel(condition, chunks, last, near_ref, far_ref, table_ref, table_t_ref, wave_ref, *refs):
    del table_t_ref
    *_, out_ref, kept_ref, sum_ref = refs[-5:-2]
    rank, layer = position()

    @pl.when(condition(layer))
    def _():
        size = near_ref.shape[2]
        modes = out_ref.shape[0]
        waves = first_waves(wave_ref, modes)
        slices = range(CLUSTER * chunks[0], CLUSTER * chunks[1])
        for index in slices:
            at = index ^ rank
            kind, cosine, sine = patch_of(near_ref, far_ref, at, size)
            if last and index == slices[-1]:
                kind = kind + 3
            if index % 2 == 1:
                cosine, sine = cosine.T, sine.T
            high, low = table_ref[kind, 0], table_ref[kind, 1]
            slot = jnp.minimum(at, 2)
            after = []
            for m in range(modes):
                real, imag = waves[m][:, :size], waves[m][:, size:]
                u = jnp.concatenate(
                    [cosine * real - sine * imag, cosine * imag + sine * real], axis=1
                )
                kept_ref[slot, m] = u
                after.append(two_sided(u, high, low, size))
            waves = after
        total = None
        for m in range(modes):
            out_ref[m] = waves[m]
            if last:
                real, imag = waves[m][:, :size], waves[m][:, size:]
                power = real * real + imag * imag
                total = power if total is None else total + power
        if last:
            sum_ref[...] = total


def backward_kernel(chunk, last, near_ref, far_ref, table_ref, kept_ref, *refs):
    if last:
        mine_ref, theirs_ref, measured_ref, wave_ref, out_ref, ours_ref, _, update = refs
    else:
        _, wave_ref, out_ref, ours_ref, _, update = refs
    rank, layer = position()

    @pl.when(layer <= chunk)
    def _():
        size = near_ref.shape[2]
        modes = wave_ref.shape[0]
        waves = [wave_ref[m] for m in range(modes)]
        if last:
            misfit = mine_ref[...] + theirs_ref[...] - measured_ref[0]
            misfit = jnp.concatenate([misfit, misfit], axis=1)
            waves = [wave * misfit for wave in waves]
        slices = range(CLUSTER * chunk, CLUSTER * (chunk + 1))
        for index in reversed(slices):
            at = index ^ rank
            kind, cosine, sine = patch_of(near_ref, far_ref, at, size)
            if last and index == slices[-1]:
                kind = kind + 3
            if index % 2 == 1:
                cosine, sine = cosine.T, sine.T
            high, low = table_ref[kind, 0], table_ref[kind, 1]
            slot = jnp.minimum(at, 2)
            after = []
            gradient = None
            for m in range(modes):
                mu = two_sided(waves[m], high, low, size)
                real, imag = mu[:, :size], mu[:, size:]
                u = kept_ref[slot, m]
                term = imag * u[:, :size] - real * u[:, size:]
                gradient = term if gradient is None else gradient + term
                after.append(
                    jnp.concatenate(
                        [cosine * real + sine * imag, cosine * imag - sine * real], axis=1
                    )
                )
            update[slot] = gradient.T if index % 2 == 1 else gradient
            waves = after
        if chunk > 0:
            for m in range(modes):
                out_ref[m] = waves[m]
        ours_ref[0] = update[0]
        ours_ref[1] = update[1]


def choose_kernel(ours_ref, own_ref, other_ref):
    own_ref[...] = ours_ref[0]
    other_ref[...] = ours_ref[1]


def joined_kernel(*refs):
    del refs


def after(block, *others):
    return pl.pallas_call(
        joined_kernel,
        in_specs=[ANY] * (1 + len(others)),
        out_specs=ANY,
        out_shape=jax.ShapeDtypeStruct(block.shape, block.dtype),
        input_output_aliases={0: 0},
        compiler_params=pltpu.CompilerParams(vmem_limit_bytes=2**20),
    )(block, *others)


def shaped(*shape, dtype=F32):
    return jax.ShapeDtypeStruct(shape, dtype)


def call(kernel, ins, outs, out_specs=None, scratch=(), flops=0, limit=LIMIT, **more):
    return pl.pallas_call(
        kernel,
        in_specs=ins,
        out_specs=out_specs or [VMEM] * len(outs),
        out_shape=outs,
        scratch_shapes=list(scratch),
        compiler_params=pltpu.CompilerParams(vmem_limit_bytes=limit),
        cost_estimate=pl.CostEstimate(flops=flops, bytes_accessed=1024, transcendentals=0),
        **more,
    )


def local(potential, thickness, propagator_phase, probe, offsets, measured):
    size = probe.shape[2]
    modes = probe.shape[1] // 2
    length = lax.axis_size("slc")
    chunks = length // CLUSTER
    wave = shaped(modes, size, 2 * size)
    kept_shape = shaped(3, modes, size, 2 * size)
    panel = shaped(size, size)
    pair = shaped(2, size, size)
    table = shaped(6, 2, 2 * size, 2 * size, dtype=BF16)
    dma = pltpu.SemaphoreType.DMA
    window = pltpu.VMEM((size + 8, 2 * size), F32)

    def flipped(block, bit):
        return lax.ppermute(block, "slc", [(i, i ^ bit) for i in range(length)])

    (message,) = call(
        extract_kernel,
        [HBM, HBM, HBM],
        [shaped(size + 8, size)],
        None,
        [window, pltpu.SMEM((1, 2), jnp.int32), pltpu.SMEM((1,), jnp.int32), dma((3,))],
        limit=63 * 2**20,
    )(offsets, thickness, potential)
    received = flipped(message, 2)
    forward_table, backward_table, zeros = call(
        table_kernel,
        [VMEM],
        [table, table, shaped(*potential.shape)],
        [VMEM, VMEM, HBM],
        [pltpu.VMEM((size, potential.shape[2]), F32), dma((potential.shape[1] // size,))],
    )(propagator_phase.reshape(1, size))
    near = jnp.stack([message, after(received, forward_table)])
    far = flipped(near, 1)
    direct = [near] + [flipped(near, CLUSTER * k) for k in range(1, 2)]
    halves = [flipped(message, CLUSTER * k) for k in range(2, chunks)]

    def forward(condition, span, near, far, tables, waves, kept, power):
        last = span[1] == chunks
        ins = [near, far, *tables] + ([probe] if span[0] == 0 else [])
        aliases = {}
        if kept is not None:
            aliases = {len(ins) + k: k for k in range(3)}
            ins += [waves, kept, power]
        *results, first, second = call(
            functools.partial(forward_kernel, condition, span, last),
            [VMEM] * len(ins),
            [wave, kept_shape, panel, table, table],
            None,
            input_output_aliases=aliases | {2: 3, 3: 4},
        )(*ins)
        return (first, second), *results

    tables = (forward_table, backward_table)
    tables, waves, kept, power = forward(
        lambda layer: layer == 0, (0, 1), near, far, tables, None, None, None
    )
    halves = jnp.stack(halves)
    crossed = after(flipped(halves, 2), waves)
    late = [block for k in range(chunks - 2) for block in (halves[k], crossed[k])]
    blocks = jnp.concatenate([near, after(direct[1], waves), jnp.stack(late)])
    others = flipped(blocks, 1)
    tables, waves, kept, power = forward(
        lambda layer: layer > 0, (0, 1), blocks, others, tables, waves, kept, power
    )
    for start in range(1, chunks, 3):
        tables, waves, kept, power = forward(
            lambda layer: layer >= 0,
            (start, min(start + 3, chunks)),
            blocks,
            others,
            tables,
            waves,
            kept,
            power,
        )
    backward_table = tables[1]
    ours = None
    extra = (power, flipped(power, 1), measured)
    for chunk in reversed(range(chunks)):
        last = chunk == chunks - 1
        ins = [blocks, others, backward_table, kept, *(extra if last else (ours,)), waves]
        aliases = {2: 2, len(ins) - 1: 0}
        if not last:
            aliases[4] = 1
        waves, ours, backward_table = call(
            functools.partial(backward_kernel, chunk, last),
            [VMEM] * len(ins),
            [wave, pair, table],
            None,
            [pltpu.VMEM((3, size, size), F32)],
            input_output_aliases=aliases,
        )(*ins)
    own, other = call(choose_kernel, [VMEM], [panel, panel])(ours)
    (gradient,) = call(
        place_kernel,
        [SMEM, VMEM, VMEM, HBM],
        [shaped(*potential.shape)],
        [HBM],
        [window, dma],
        input_output_aliases={3: 0},
    )(offsets, own, flipped(other, 1), zeros)
    return gradient


def solution(mesh):
    placed = (
        P(("grp", "slc"), None, None),
        P(("grp", "slc")),
        P(),
        P("grp", None, None, None),
        P("grp", None),
        P("grp", None, None),
    )
    return jax.shard_map(
        local, mesh=mesh, in_specs=placed, out_specs=P(("grp", "slc"), None, None), check_vma=False
    )
```

```python
import functools
import math

import jax
import jax.numpy as jnp
from jax import lax
from jax.experimental import pallas as pl
from jax.experimental.pallas import tpu as pltpu
from jax.sharding import PartitionSpec as P

F32 = jnp.float32
BF16 = jnp.bfloat16
CLUSTER = 4
LIMIT = 12 * 2**20
VMEM = pl.BlockSpec(memory_space=pltpu.VMEM)
SMEM = pl.BlockSpec(memory_space=pltpu.SMEM)
HBM = pl.BlockSpec(memory_space=pltpu.HBM)
ANY = pl.BlockSpec(memory_space=pl.ANY)


def sincos(x):
    turns = jnp.floor(x * (2.0 / math.pi) + 0.5)
    r = x - turns * 1.5703125
    r = r - turns * 4.837512969970703125e-4
    r = r - turns * 7.549789948768648e-8
    r2 = r * r
    s = r + r * r2 * (-1.6666654611e-1 + r2 * (8.3321608736e-3 + r2 * -1.9515295891e-4))
    c = 1.0 - 0.5 * r2 + r2 * r2 * (
        4.166664568298827e-2 + r2 * (-1.388731625493765e-3 + r2 * 2.443315711809948e-5)
    )
    quadrant = turns.astype(jnp.int32)
    odd = (quadrant & 1) == 1
    sine = jnp.where(odd, c, s)
    cosine = jnp.where(odd, s, c)
    sine = jnp.where((quadrant & 2) == 2, -sine, sine)
    cosine = jnp.where(((quadrant + 1) & 2) == 2, -cosine, cosine)
    return cosine, sine


def split(x):
    high = x.astype(BF16)
    return high, (x - high.astype(F32)).astype(BF16)


def dot(a, b):
    return jnp.dot(a, b, preferred_element_type=F32)


def product(x, high, low):
    x_high, x_low = split(x)
    return dot(x_high, high) + dot(x_low, high) + dot(x_high, low)


def turned(x, size):
    return jnp.concatenate([x[:, :size].T, x[:, size:].T], axis=1)


def two_sided(x, high, low, size):
    return product(turned(product(x, high, low), size), high, low)


def window_of(offsets_ref, rows, columns, size):
    row, column = offsets_ref[0, 0], offsets_ref[0, 1]
    row_base = jnp.minimum(row // 8 * 8, rows - size - 8)
    column_base = jnp.minimum(column // 128 * 128, columns - 2 * size)
    return (
        pl.multiple_of(row_base, 8),
        pl.multiple_of(column_base, 128),
        row - row_base,
        column - column_base,
    )


def extract_kernel(offsets_hbm, thickness_hbm, potential_ref, out_ref, window, offsets_ref, thickness_ref, sems):
    size = out_ref.shape[1]
    corner = pltpu.make_async_copy(offsets_hbm, offsets_ref, sems.at[0])
    steps = pltpu.make_async_copy(thickness_hbm, thickness_ref, sems.at[1])
    corner.start()
    steps.start()
    corner.wait()
    row_base, column_base, down, across = window_of(
        offsets_ref, potential_ref.shape[1], potential_ref.shape[2], size
    )
    copy = pltpu.make_async_copy(
        potential_ref.at[0, pl.ds(row_base, size + 8), pl.ds(column_base, 2 * size)], window, sems.at[2]
    )
    copy.start()
    steps.wait()
    out_ref[size:, :] = jnp.full((8, size), thickness_ref[0].astype(F32))
    copy.wait()
    part = pltpu.roll(window[...], lax.rem(size + 8 - down, size + 8), 0)[:size]
    shift = lax.rem(size - across, size)
    left = pltpu.roll(part[:, :size], shift, 1)
    right = pltpu.roll(part[:, size:], shift, 1)
    lane = lax.broadcasted_iota(jnp.int32, (size, size), 1)
    out_ref[:size, :] = jnp.where(lane < size - across, left, right)


def place_kernel(offsets_ref, ours_ref, theirs_ref, zeros_ref, out_ref, window, sem):
    del zeros_ref
    size = theirs_ref.shape[1]
    row_base, column_base, down, across = window_of(
        offsets_ref, out_ref.shape[1], out_ref.shape[2], size
    )
    update = jnp.concatenate([ours_ref[...] + theirs_ref[...], jnp.zeros((8, size), F32)], axis=0)
    update = pltpu.roll(pltpu.roll(update, down, 0), lax.rem(across, size), 1)
    lane = lax.broadcasted_iota(jnp.int32, (size + 8, size), 1)
    window[:, :size] = jnp.where(lane < across, 0.0, update)
    window[:, size:] = jnp.where(lane < across, update, 0.0)
    copy = pltpu.make_async_copy(
        window, out_ref.at[0, pl.ds(row_base, size + 8), pl.ds(column_base, 2 * size)], sem
    )
    copy.start()
    copy.wait()


def table_kernel(phase_ref, forward_ref, backward_ref, zeros_ref, blank, sem):
    size = phase_ref.shape[1]
    blank[...] = jnp.zeros_like(blank)
    copies = [
        pltpu.make_async_copy(blank, zeros_ref.at[0, pl.ds(row, size)], sem.at[k])
        for k, row in enumerate(range(0, zeros_ref.shape[1], size))
    ]
    for copy in copies:
        copy.start()
    rows = lax.broadcasted_iota(jnp.int32, (size, size), 0)
    columns = lax.broadcasted_iota(jnp.int32, (size, size), 1)
    angle = ((rows * columns) % size).astype(F32) * (2.0 * math.pi / size)
    c, s = sincos(angle)
    whole = jnp.concatenate(
        [jnp.concatenate([c, s], axis=1), jnp.concatenate([-s, c], axis=1)], axis=0
    )

    def put(index, real, imag):
        real_turned, imag_turned = real.T, imag.T
        for ref, quarters in (
            (forward_ref, (real, imag, -imag, real)),
            (backward_ref, (real_turned, -imag_turned, imag_turned, real_turned)),
        ):
            for place, quarter in enumerate(quarters):
                r, k = place // 2 * size, place % 2 * size
                high, low = split(quarter)
                ref[index, 0, r : r + size, k : k + size] = high
                ref[index, 1, r : r + size, k : k + size] = low

    for steps in (1, 2, 3):
        h_real, h_imag = sincos(phase_ref[...] * float(steps))
        real = c * h_real + s * h_imag
        imag = c * h_imag - s * h_real
        put(2 + steps, real * (1.0 / math.sqrt(size)), imag * (1.0 / math.sqrt(size)))
        both = jnp.concatenate([real, imag], axis=1)
        k = jnp.dot(both, whole, precision=lax.Precision.HIGHEST, preferred_element_type=F32)
        put(steps - 1, k[:, :size] * (1.0 / size), k[:, size:] * (1.0 / size))
    for copy in copies:
        copy.wait()


def steps_of(ref, index, size):
    steps = ref[index, size, 0].astype(jnp.int32)
    return jnp.clip(steps, 1, 3) - 1


def position():
    rank = lax.axis_index("slc")
    return rank, rank // CLUSTER


def patch_of(near_ref, far_ref, at, size):
    block, half, crossed = at // CLUSTER, (at // 2) % 2, at % 2 == 1
    entry = 2 * block + half
    steps = jnp.where(crossed, far_ref[entry, size, 0], near_ref[entry, size, 0])
    kind = jnp.clip(steps.astype(jnp.int32), 1, 3) - 1
    cosine, sine = sincos(jnp.where(crossed, far_ref[entry, :size, :], near_ref[entry, :size, :]))
    return kind, cosine, sine


def first_waves(wave_ref, modes):
    if wave_ref.dtype == F32:
        return [wave_ref[m] for m in range(modes)]
    start = (lax.axis_index("slc") % 2) * modes
    return [
        jnp.concatenate(
            [wave_ref[0, start + m].astype(F32), wave_ref[1, start + m].astype(F32)], axis=1
        )
        for m in range(modes)
    ]


def forward_kernel(condition, chunks, last, near_ref, far_ref, table_ref, table_t_ref, wave_ref, *refs):
    del table_t_ref
    *_, out_ref, kept_ref, sum_ref = refs[-5:-2]
    rank, layer = position()

    size = near_ref.shape[2]
    modes = out_ref.shape[0]

    def run():
        waves = first_waves(wave_ref, modes)
        slices = range(CLUSTER * chunks[0], CLUSTER * chunks[1])
        for index in slices:
            at = index ^ rank
            kind, cosine, sine = patch_of(near_ref, far_ref, at, size)
            if last and index == slices[-1]:
                kind = kind + 3
            if index % 2 == 1:
                cosine, sine = cosine.T, sine.T
            high, low = table_ref[kind, 0], table_ref[kind, 1]
            slot = jnp.minimum(at, 2)
            after = []
            for m in range(modes):
                real, imag = waves[m][:, :size], waves[m][:, size:]
                u = jnp.concatenate(
                    [cosine * real - sine * imag, cosine * imag + sine * real], axis=1
                )
                kept_ref[slot, m] = u
                after.append(two_sided(u, high, low, size))
            waves = after
        total = None
        for m in range(modes):
            out_ref[m] = waves[m]
            if last:
                real, imag = waves[m][:, :size], waves[m][:, size:]
                power = real * real + imag * imag
                total = power if total is None else total + power
        if last:
            sum_ref[...] = total

    pl.when(condition(layer))(run)


def backward_kernel(chunk, last, near_ref, far_ref, table_ref, kept_ref, *refs):
    if last:
        mine_ref, theirs_ref, measured_ref, *refs = refs
    else:
        refs = refs[1:]
    wave_ref, *outs, ours_ref, _, update = refs
    rank, layer = position()

    size = near_ref.shape[2]
    modes = wave_ref.shape[0]

    def run():
        waves = [wave_ref[m] for m in range(modes)]
        if last:
            misfit = mine_ref[...] + theirs_ref[...] - measured_ref[0]
            misfit = jnp.concatenate([misfit, misfit], axis=1)
            waves = [wave * misfit for wave in waves]
        slices = range(CLUSTER * chunk, CLUSTER * (chunk + 1))
        for index in reversed(slices):
            at = index ^ rank
            kind, cosine, sine = patch_of(near_ref, far_ref, at, size)
            if last and index == slices[-1]:
                kind = kind + 3
            if index % 2 == 1:
                cosine, sine = cosine.T, sine.T
            high, low = table_ref[kind, 0], table_ref[kind, 1]
            slot = jnp.minimum(at, 2)
            after = []
            gradient = None
            for m in range(modes):
                mu = two_sided(waves[m], high, low, size)
                real, imag = mu[:, :size], mu[:, size:]
                u = kept_ref[slot, m]
                term = imag * u[:, :size] - real * u[:, size:]
                gradient = term if gradient is None else gradient + term
                if index > 0:
                    after.append(
                        jnp.concatenate(
                            [cosine * real + sine * imag, cosine * imag - sine * real], axis=1
                        )
                    )
            update[slot] = gradient.T if index % 2 == 1 else gradient
            waves = after
        ours_ref[0] = update[0]
        ours_ref[1] = update[1]
        for out_ref in outs:
            for m, wave in enumerate(waves):
                out_ref[m] = wave

    pl.when(layer <= chunk)(run)


def choose_kernel(ours_ref, own_ref, other_ref):
    own_ref[...] = ours_ref[0]
    other_ref[...] = ours_ref[1]


def joined_kernel(*refs):
    del refs


def after(block, *others):
    return pl.pallas_call(
        joined_kernel,
        in_specs=[ANY] * (1 + len(others)),
        out_specs=ANY,
        out_shape=jax.ShapeDtypeStruct(block.shape, block.dtype),
        input_output_aliases={0: 0},
        compiler_params=pltpu.CompilerParams(vmem_limit_bytes=2**20),
    )(block, *others)


def shaped(*shape, dtype=F32):
    return jax.ShapeDtypeStruct(shape, dtype)


def call(kernel, ins, outs, out_specs=None, scratch=(), flops=0, limit=LIMIT, **more):
    return pl.pallas_call(
        kernel,
        in_specs=ins,
        out_specs=out_specs or [VMEM] * len(outs),
        out_shape=outs,
        scratch_shapes=list(scratch),
        compiler_params=pltpu.CompilerParams(vmem_limit_bytes=limit),
        cost_estimate=pl.CostEstimate(flops=flops, bytes_accessed=1024, transcendentals=0),
        **more,
    )


def local(potential, thickness, propagator_phase, probe, offsets, measured):
    size = probe.shape[2]
    modes = probe.shape[1] // 2
    length = lax.axis_size("slc")
    chunks = length // CLUSTER
    wave = shaped(modes, size, 2 * size)
    kept_shape = shaped(3, modes, size, 2 * size)
    panel = shaped(size, size)
    pair = shaped(2, size, size)
    table = shaped(6, 2, 2 * size, 2 * size, dtype=BF16)
    dma = pltpu.SemaphoreType.DMA
    window = pltpu.VMEM((size + 8, 2 * size), F32)

    def flipped(block, bit):
        return lax.ppermute(block, "slc", [(i, i ^ bit) for i in range(length)])

    (message,) = call(
        extract_kernel,
        [HBM, HBM, HBM],
        [shaped(size + 8, size)],
        None,
        [window, pltpu.SMEM((1, 2), jnp.int32), pltpu.SMEM((1,), jnp.int32), dma((3,))],
        limit=63 * 2**20,
    )(offsets, thickness, potential)
    received = flipped(message, 2)
    forward_table, backward_table, zeros = call(
        table_kernel,
        [VMEM],
        [table, table, shaped(*potential.shape)],
        [VMEM, VMEM, HBM],
        [pltpu.VMEM((size, potential.shape[2]), F32), dma((potential.shape[1] // size,))],
    )(propagator_phase.reshape(1, size))
    near = jnp.stack([message, after(received, forward_table)])
    far = flipped(near, 1)
    beside = flipped(near, CLUSTER)
    halves = [flipped(message, CLUSTER * k) for k in range(2, chunks)]
    crossed = [flipped(half, 2) for half in halves]

    def forward(condition, span, near, far, tables, waves, kept, power):
        last = span[1] == chunks
        ins = [near, far, *tables] + ([probe] if span[0] == 0 else [])
        aliases = {}
        if kept is not None:
            aliases = {len(ins) + k: k for k in range(3)}
            ins += [waves, kept, power]
        *results, first, second = call(
            functools.partial(forward_kernel, condition, span, last),
            [VMEM] * len(ins),
            [wave, kept_shape, panel, table, table],
            None,
            input_output_aliases=aliases | {2: 3, 3: 4},
        )(*ins)
        return (first, second), *results

    tables = (forward_table, backward_table)
    state = forward(lambda layer: layer == 0, (0, 1), near, far, tables, None, None, None)
    beside = after(beside, state[1])
    early = (jnp.concatenate([near, beside]), jnp.concatenate([far, flipped(beside, 1)]))
    late = [block for half, cross in zip(halves, crossed) for block in (half, after(cross, state[1]))]
    late = jnp.stack(late)
    late_far = flipped(late, 1)
    state = forward(lambda layer: layer == 1, (0, 1), *early, *state)
    state = forward(lambda layer: layer <= 1, (1, 2), *early, *state)
    blocks = jnp.concatenate([early[0], late])
    others = jnp.concatenate([early[1], after(late_far, state[1])])
    state = forward(lambda layer: layer > 1, (0, 2), blocks, others, *state)
    for start in range(2, chunks, 2):
        span = (start, min(start + 2, chunks))
        state = forward(lambda layer: layer >= 0, span, blocks, others, *state)
    tables, waves, kept, power = state
    backward_table = tables[1]
    ours, waves = None, [waves]
    extra = (power, flipped(power, 1), measured)
    for chunk in reversed(range(chunks)):
        last = chunk == chunks - 1
        ins = [blocks, others, backward_table, kept, *(extra if last else (ours,)), *waves]
        outs = [wave] if chunk > 0 else []
        aliases = {2: len(outs) + 1}
        if not last:
            aliases[4] = len(outs)
        if outs:
            aliases[len(ins) - 1] = 0
        *waves, ours, backward_table = call(
            functools.partial(backward_kernel, chunk, last),
            [VMEM] * len(ins),
            outs + [pair, table],
            None,
            [pltpu.VMEM((3, size, size), F32)],
            input_output_aliases=aliases,
        )(*ins)
    own, other = call(choose_kernel, [VMEM], [panel, panel])(ours)
    (gradient,) = call(
        place_kernel,
        [VMEM, VMEM, VMEM, HBM],
        [shaped(*potential.shape)],
        [HBM],
        [window, dma],
        input_output_aliases={3: 0},
    )(offsets, own, flipped(other, 1), zeros)
    return gradient


def solution(mesh):
    placed = (
        P(("grp", "slc"), None, None),
        P(("grp", "slc")),
        P(),
        P("grp", None, None, None),
        P("grp", None),
        P("grp", None, None),
    )
    return jax.shard_map(
        local, mesh=mesh, in_specs=placed, out_specs=P(("grp", "slc"), None, None), check_vma=False
    )
```

```python
import functools
import math

import jax
import jax.numpy as jnp
from jax import lax
from jax.experimental import pallas as pl
from jax.experimental.pallas import tpu as pltpu
from jax.sharding import PartitionSpec as P

F32 = jnp.float32
BF16 = jnp.bfloat16
CLUSTER = 4
LIMIT = 12 * 2**20
VMEM = pl.BlockSpec(memory_space=pltpu.VMEM)
SMEM = pl.BlockSpec(memory_space=pltpu.SMEM)
HBM = pl.BlockSpec(memory_space=pltpu.HBM)
ANY = pl.BlockSpec(memory_space=pl.ANY)


def sincos(x):
    turns = jnp.floor(x * (2.0 / math.pi) + 0.5)
    r = x - turns * 1.5703125
    r = r - turns * 4.837512969970703125e-4
    r = r - turns * 7.549789948768648e-8
    r2 = r * r
    s = r + r * r2 * (-1.6666654611e-1 + r2 * (8.3321608736e-3 + r2 * -1.9515295891e-4))
    c = 1.0 - 0.5 * r2 + r2 * r2 * (
        4.166664568298827e-2 + r2 * (-1.388731625493765e-3 + r2 * 2.443315711809948e-5)
    )
    quadrant = turns.astype(jnp.int32)
    odd = (quadrant & 1) == 1
    sine = jnp.where(odd, c, s)
    cosine = jnp.where(odd, s, c)
    sine = jnp.where((quadrant & 2) == 2, -sine, sine)
    cosine = jnp.where(((quadrant + 1) & 2) == 2, -cosine, cosine)
    return cosine, sine


def split(x):
    high = x.astype(BF16)
    return high, (x - high.astype(F32)).astype(BF16)


def dot(a, b):
    return jnp.dot(a, b, preferred_element_type=F32)


def product(x, high, low):
    x_high, x_low = split(x)
    return dot(x_high, high) + dot(x_low, high) + dot(x_high, low)


def turned(x, size):
    return jnp.concatenate([x[:, :size].T, x[:, size:].T], axis=1)


def two_sided(x, high, low, size):
    return product(turned(product(x, high, low), size), high, low)


def window_of(offsets_ref, rows, columns, size):
    row, column = offsets_ref[0, 0], offsets_ref[0, 1]
    row_base = jnp.minimum(row // 8 * 8, rows - size - 8)
    column_base = jnp.minimum(column // 128 * 128, columns - 2 * size)
    return (
        pl.multiple_of(row_base, 8),
        pl.multiple_of(column_base, 128),
        row - row_base,
        column - column_base,
    )


def extract_kernel(
    offsets_hbm, thickness_hbm, phase_hbm, potential_ref, out_ref, window, offsets_ref, thickness_ref, phase_ref, sems
):
    size = out_ref.shape[1]
    phases = pltpu.make_async_copy(phase_hbm, phase_ref, sems.at[3])
    phases.start()
    corner = pltpu.make_async_copy(offsets_hbm, offsets_ref, sems.at[0])
    steps = pltpu.make_async_copy(thickness_hbm, thickness_ref, sems.at[1])
    corner.start()
    steps.start()
    corner.wait()
    row_base, column_base, down, across = window_of(
        offsets_ref, potential_ref.shape[1], potential_ref.shape[2], size
    )
    copy = pltpu.make_async_copy(
        potential_ref.at[0, pl.ds(row_base, size + 8), pl.ds(column_base, 2 * size)], window, sems.at[2]
    )
    copy.start()
    steps.wait()
    phases.wait()
    row = lax.broadcasted_iota(jnp.int32, (8, size), 0)
    out_ref[size:, :] = jnp.where(row == 1, phase_ref[...], thickness_ref[0].astype(F32))
    copy.wait()
    part = pltpu.roll(window[...], lax.rem(size + 8 - down, size + 8), 0)[:size]
    shift = lax.rem(size - across, size)
    left = pltpu.roll(part[:, :size], shift, 1)
    right = pltpu.roll(part[:, size:], shift, 1)
    lane = lax.broadcasted_iota(jnp.int32, (size, size), 1)
    out_ref[:size, :] = jnp.where(lane < size - across, left, right)


def place_kernel(offsets_ref, ours_ref, theirs_ref, zeros_ref, out_ref, window, sem):
    del zeros_ref
    size = theirs_ref.shape[1]
    row_base, column_base, down, across = window_of(
        offsets_ref, out_ref.shape[1], out_ref.shape[2], size
    )
    update = jnp.concatenate([ours_ref[...] + theirs_ref[...], jnp.zeros((8, size), F32)], axis=0)
    update = pltpu.roll(pltpu.roll(update, down, 0), lax.rem(across, size), 1)
    lane = lax.broadcasted_iota(jnp.int32, (size + 8, size), 1)
    window[:, :size] = jnp.where(lane < across, 0.0, update)
    window[:, size:] = jnp.where(lane < across, update, 0.0)
    copy = pltpu.make_async_copy(
        window, out_ref.at[0, pl.ds(row_base, size + 8), pl.ds(column_base, 2 * size)], sem
    )
    copy.start()
    copy.wait()


def table_kernel(message_ref, forward_ref, backward_ref, zeros_ref, blank, sem):
    size = message_ref.shape[1]
    blank[...] = jnp.zeros_like(blank)
    copies = [
        pltpu.make_async_copy(blank, zeros_ref.at[0, pl.ds(row, size)], sem.at[k])
        for k, row in enumerate(range(0, zeros_ref.shape[1], size))
    ]
    for copy in copies:
        copy.start()
    rows = lax.broadcasted_iota(jnp.int32, (size, size), 0)
    columns = lax.broadcasted_iota(jnp.int32, (size, size), 1)
    angle = ((rows * columns) % size).astype(F32) * (2.0 * math.pi / size)
    c, s = sincos(angle)
    whole = jnp.concatenate(
        [jnp.concatenate([c, s], axis=1), jnp.concatenate([-s, c], axis=1)], axis=0
    )

    def put(index, real, imag):
        real_turned, imag_turned = real.T, imag.T
        for ref, quarters in (
            (forward_ref, (real, imag, -imag, real)),
            (backward_ref, (real_turned, -imag_turned, imag_turned, real_turned)),
        ):
            for place, quarter in enumerate(quarters):
                r, k = place // 2 * size, place % 2 * size
                high, low = split(quarter)
                ref[index, 0, r : r + size, k : k + size] = high
                ref[index, 1, r : r + size, k : k + size] = low

    for steps in (1, 2, 3):
        h_real, h_imag = sincos(message_ref[size + 1 : size + 2, :] * float(steps))
        real = c * h_real + s * h_imag
        imag = c * h_imag - s * h_real
        put(2 + steps, real * (1.0 / math.sqrt(size)), imag * (1.0 / math.sqrt(size)))
        both = jnp.concatenate([real, imag], axis=1)
        k = jnp.dot(both, whole, precision=lax.Precision.HIGHEST, preferred_element_type=F32)
        put(steps - 1, k[:, :size] * (1.0 / size), k[:, size:] * (1.0 / size))
    for copy in copies:
        copy.wait()


def steps_of(ref, index, size):
    steps = ref[index, size, 0].astype(jnp.int32)
    return jnp.clip(steps, 1, 3) - 1


def position():
    rank = lax.axis_index("slc")
    return rank, rank // CLUSTER


def patch_of(near_ref, far_ref, at, size):
    block, half, crossed = at // CLUSTER, (at // 2) % 2, at % 2 == 1
    entry = 2 * block + half
    steps = jnp.where(crossed, far_ref[entry, size, 0], near_ref[entry, size, 0])
    kind = jnp.clip(steps.astype(jnp.int32), 1, 3) - 1
    cosine, sine = sincos(jnp.where(crossed, far_ref[entry, :size, :], near_ref[entry, :size, :]))
    return kind, cosine, sine


def first_waves(wave_ref, modes):
    if wave_ref.dtype == F32:
        return [wave_ref[m] for m in range(modes)]
    start = (lax.axis_index("slc") % 2) * modes
    return [
        jnp.concatenate(
            [wave_ref[0, start + m].astype(F32), wave_ref[1, start + m].astype(F32)], axis=1
        )
        for m in range(modes)
    ]


def forward_kernel(condition, chunks, last, near_ref, far_ref, table_ref, table_t_ref, wave_ref, *refs):
    del table_t_ref
    *_, out_ref, kept_ref, sum_ref = refs[-5:-2]
    rank, layer = position()

    size = near_ref.shape[2]
    modes = out_ref.shape[0]

    def run():
        waves = first_waves(wave_ref, modes)
        slices = range(CLUSTER * chunks[0], CLUSTER * chunks[1])
        for index in slices:
            at = index ^ rank
            kind, cosine, sine = patch_of(near_ref, far_ref, at, size)
            if last and index == slices[-1]:
                kind = kind + 3
            if index % 2 == 1:
                cosine, sine = cosine.T, sine.T
            high, low = table_ref[kind, 0], table_ref[kind, 1]
            slot = jnp.minimum(at, 2)
            after = []
            for m in range(modes):
                real, imag = waves[m][:, :size], waves[m][:, size:]
                u = jnp.concatenate(
                    [cosine * real - sine * imag, cosine * imag + sine * real], axis=1
                )
                kept_ref[slot, m] = u
                after.append(two_sided(u, high, low, size))
            waves = after
        total = None
        for m in range(modes):
            out_ref[m] = waves[m]
            if last:
                real, imag = waves[m][:, :size], waves[m][:, size:]
                power = real * real + imag * imag
                total = power if total is None else total + power
        if last:
            sum_ref[...] = total

    pl.when(condition(layer))(run)


def backward_kernel(chunk, last, near_ref, far_ref, table_ref, kept_ref, *refs):
    if last:
        mine_ref, theirs_ref, measured_ref, *refs = refs
    else:
        refs = refs[1:]
    wave_ref, *outs, ours_ref, _, update = refs
    rank, layer = position()

    size = near_ref.shape[2]
    modes = wave_ref.shape[0]

    def run():
        waves = [wave_ref[m] for m in range(modes)]
        if last:
            misfit = mine_ref[...] + theirs_ref[...] - measured_ref[0]
            misfit = jnp.concatenate([misfit, misfit], axis=1)
            waves = [wave * misfit for wave in waves]
        slices = range(CLUSTER * chunk, CLUSTER * (chunk + 1))
        for index in reversed(slices):
            at = index ^ rank
            kind, cosine, sine = patch_of(near_ref, far_ref, at, size)
            if last and index == slices[-1]:
                kind = kind + 3
            if index % 2 == 1:
                cosine, sine = cosine.T, sine.T
            high, low = table_ref[kind, 0], table_ref[kind, 1]
            slot = jnp.minimum(at, 2)
            after = []
            gradient = None
            for m in range(modes):
                mu = two_sided(waves[m], high, low, size)
                real, imag = mu[:, :size], mu[:, size:]
                u = kept_ref[slot, m]
                term = imag * u[:, :size] - real * u[:, size:]
                gradient = term if gradient is None else gradient + term
                if index > 0:
                    after.append(
                        jnp.concatenate(
                            [cosine * real + sine * imag, cosine * imag - sine * real], axis=1
                        )
                    )
            update[slot] = gradient.T if index % 2 == 1 else gradient
            waves = after
        ours_ref[0] = update[0]
        ours_ref[1] = update[1]
        for out_ref in outs:
            for m, wave in enumerate(waves):
                out_ref[m] = wave

    pl.when(layer <= chunk)(run)


def choose_kernel(ours_ref, own_ref, other_ref):
    own_ref[...] = ours_ref[0]
    other_ref[...] = ours_ref[1]


def joined_kernel(*refs):
    del refs


def after(block, *others):
    return pl.pallas_call(
        joined_kernel,
        in_specs=[ANY] * (1 + len(others)),
        out_specs=ANY,
        out_shape=jax.ShapeDtypeStruct(block.shape, block.dtype),
        input_output_aliases={0: 0},
        compiler_params=pltpu.CompilerParams(vmem_limit_bytes=2**20),
    )(block, *others)


def shaped(*shape, dtype=F32):
    return jax.ShapeDtypeStruct(shape, dtype)


def call(kernel, ins, outs, out_specs=None, scratch=(), flops=0, limit=LIMIT, **more):
    return pl.pallas_call(
        kernel,
        in_specs=ins,
        out_specs=out_specs or [VMEM] * len(outs),
        out_shape=outs,
        scratch_shapes=list(scratch),
        compiler_params=pltpu.CompilerParams(vmem_limit_bytes=limit),
        cost_estimate=pl.CostEstimate(flops=flops, bytes_accessed=1024, transcendentals=0),
        **more,
    )


def local(potential, thickness, propagator_phase, probe, offsets, measured):
    size = probe.shape[2]
    modes = probe.shape[1] // 2
    length = lax.axis_size("slc")
    chunks = length // CLUSTER
    wave = shaped(modes, size, 2 * size)
    kept_shape = shaped(3, modes, size, 2 * size)
    panel = shaped(size, size)
    pair = shaped(2, size, size)
    table = shaped(6, 2, 2 * size, 2 * size, dtype=BF16)
    dma = pltpu.SemaphoreType.DMA
    window = pltpu.VMEM((size + 8, 2 * size), F32)

    def flipped(block, bit):
        return lax.ppermute(block, "slc", [(i, i ^ bit) for i in range(length)])

    (message,) = call(
        extract_kernel,
        [HBM, HBM, HBM, HBM],
        [shaped(size + 8, size)],
        None,
        [
            window,
            pltpu.SMEM((1, 2), jnp.int32),
            pltpu.SMEM((1,), jnp.int32),
            pltpu.VMEM((1, size), F32),
            dma((4,)),
        ],
        limit=63 * 2**20,
    )(offsets, thickness, propagator_phase.reshape(1, size), potential)
    received = flipped(message, 2)
    forward_table, backward_table, zeros = call(
        table_kernel,
        [VMEM],
        [table, table, shaped(*potential.shape)],
        [VMEM, VMEM, HBM],
        [pltpu.VMEM((size, potential.shape[2]), F32), dma((potential.shape[1] // size,))],
    )(message)
    near = after(jnp.stack([message, received]), forward_table)
    far = flipped(near, 1)
    beside = flipped(near, CLUSTER)
    halves = [flipped(message, CLUSTER * k) for k in range(2, chunks)]
    crossed = [flipped(half, 2) for half in halves]

    def forward(condition, span, near, far, tables, waves, kept, power):
        last = span[1] == chunks
        ins = [near, far, *tables] + ([probe] if span[0] == 0 else [])
        aliases = {}
        if kept is not None:
            aliases = {len(ins) + k: k for k in range(3)}
            ins += [waves, kept, power]
        *results, first, second = call(
            functools.partial(forward_kernel, condition, span, last),
            [VMEM] * len(ins),
            [wave, kept_shape, panel, table, table],
            None,
            input_output_aliases=aliases | {2: 3, 3: 4},
        )(*ins)
        return (first, second), *results

    tables = (forward_table, backward_table)
    state = forward(lambda layer: layer == 0, (0, 1), near, far, tables, None, None, None)
    beside = after(beside, state[1])
    early = (jnp.concatenate([near, beside]), jnp.concatenate([far, flipped(beside, 1)]))
    late = [block for half, cross in zip(halves, crossed) for block in (half, after(cross, state[1]))]
    late = jnp.stack(late)
    late_far = flipped(late, 1)
    state = forward(lambda layer: layer == 1, (0, 1), *early, *state)
    state = forward(lambda layer: layer <= 1, (1, 2), *early, *state)
    blocks = jnp.concatenate([early[0], late])
    others = jnp.concatenate([early[1], after(late_far, state[1])])
    state = forward(lambda layer: layer > 1, (0, 2), blocks, others, *state)
    for start in range(2, chunks, 2):
        span = (start, min(start + 2, chunks))
        state = forward(lambda layer: layer >= 0, span, blocks, others, *state)
    tables, waves, kept, power = state
    backward_table = tables[1]
    ours, waves = None, [waves]
    extra = (power, flipped(power, 1), measured)
    for chunk in reversed(range(chunks)):
        last = chunk == chunks - 1
        ins = [blocks, others, backward_table, kept, *(extra if last else (ours,)), *waves]
        outs = [wave] if chunk > 0 else []
        aliases = {2: len(outs) + 1}
        if not last:
            aliases[4] = len(outs)
        if outs:
            aliases[len(ins) - 1] = 0
        *waves, ours, backward_table = call(
            functools.partial(backward_kernel, chunk, last),
            [VMEM] * len(ins),
            outs + [pair, table],
            None,
            [pltpu.VMEM((3, size, size), F32)],
            input_output_aliases=aliases,
        )(*ins)
    own, other = call(choose_kernel, [VMEM], [panel, panel])(ours)
    (gradient,) = call(
        place_kernel,
        [VMEM, VMEM, VMEM, HBM],
        [shaped(*potential.shape)],
        [HBM],
        [window, dma],
        input_output_aliases={3: 0},
    )(offsets, own, flipped(other, 1), zeros)
    return gradient


def solution(mesh):
    placed = (
        P(("grp", "slc"), None, None),
        P(("grp", "slc")),
        P(),
        P("grp", None, None, None),
        P("grp", None),
        P("grp", None, None),
    )
    return jax.shard_map(
        local, mesh=mesh, in_specs=placed, out_specs=P(("grp", "slc"), None, None), check_vma=False
    )
```

```python
import functools
import math

import jax
import jax.numpy as jnp
from jax import lax
from jax.experimental import pallas as pl
from jax.experimental.pallas import tpu as pltpu
from jax.sharding import PartitionSpec as P

F32 = jnp.float32
BF16 = jnp.bfloat16
CLUSTER = 4
LIMIT = 12 * 2**20
VMEM = pl.BlockSpec(memory_space=pltpu.VMEM)
SMEM = pl.BlockSpec(memory_space=pltpu.SMEM)
HBM = pl.BlockSpec(memory_space=pltpu.HBM)
ANY = pl.BlockSpec(memory_space=pl.ANY)


def sincos(x):
    turns = jnp.floor(x * (2.0 / math.pi) + 0.5)
    r = x - turns * 1.5703125
    r = r - turns * 4.837512969970703125e-4
    r = r - turns * 7.549789948768648e-8
    r2 = r * r
    s = r + r * r2 * (-1.6666654611e-1 + r2 * (8.3321608736e-3 + r2 * -1.9515295891e-4))
    c = 1.0 - 0.5 * r2 + r2 * r2 * (
        4.166664568298827e-2 + r2 * (-1.388731625493765e-3 + r2 * 2.443315711809948e-5)
    )
    quadrant = turns.astype(jnp.int32)
    odd = (quadrant & 1) == 1
    sine = jnp.where(odd, c, s)
    cosine = jnp.where(odd, s, c)
    sine = jnp.where((quadrant & 2) == 2, -sine, sine)
    cosine = jnp.where(((quadrant + 1) & 2) == 2, -cosine, cosine)
    return cosine, sine


def split(x):
    high = x.astype(BF16)
    return high, (x - high.astype(F32)).astype(BF16)


def dot(a, b):
    return jnp.dot(a, b, preferred_element_type=F32)


def product(x, high, low):
    x_high, x_low = split(x)
    return dot(x_high, high) + dot(x_low, high) + dot(x_high, low)


def turned(x, size):
    return jnp.concatenate([x[:, :size].T, x[:, size:].T], axis=1)


def two_sided(x, high, low, size):
    return product(turned(product(x, high, low), size), high, low)


def window_of(offsets_ref, rows, columns, size):
    row, column = offsets_ref[0, 0], offsets_ref[0, 1]
    row_base = jnp.minimum(row // 8 * 8, rows - size - 8)
    column_base = jnp.minimum(column // 128 * 128, columns - 2 * size)
    return (
        pl.multiple_of(row_base, 8),
        pl.multiple_of(column_base, 128),
        row - row_base,
        column - column_base,
    )


def extract_kernel(
    offsets_hbm, thickness_hbm, phase_hbm, potential_ref, out_ref, window, offsets_ref, thickness_ref, phase_ref, sems
):
    size = out_ref.shape[1]
    phases = pltpu.make_async_copy(phase_hbm, phase_ref, sems.at[3])
    phases.start()
    corner = pltpu.make_async_copy(offsets_hbm, offsets_ref, sems.at[0])
    steps = pltpu.make_async_copy(thickness_hbm, thickness_ref, sems.at[1])
    corner.start()
    steps.start()
    corner.wait()
    row_base, column_base, down, across = window_of(
        offsets_ref, potential_ref.shape[1], potential_ref.shape[2], size
    )
    copy = pltpu.make_async_copy(
        potential_ref.at[0, pl.ds(row_base, size + 8), pl.ds(column_base, 2 * size)], window, sems.at[2]
    )
    copy.start()
    steps.wait()
    phases.wait()
    row = lax.broadcasted_iota(jnp.int32, (8, size), 0)
    out_ref[size:, :] = jnp.where(row == 1, phase_ref[...], thickness_ref[0].astype(F32))
    copy.wait()
    part = pltpu.roll(window[...], lax.rem(size + 8 - down, size + 8), 0)[:size]
    shift = lax.rem(size - across, size)
    left = pltpu.roll(part[:, :size], shift, 1)
    right = pltpu.roll(part[:, size:], shift, 1)
    lane = lax.broadcasted_iota(jnp.int32, (size, size), 1)
    out_ref[:size, :] = jnp.where(lane < size - across, left, right)


def place_kernel(offsets_ref, ours_ref, theirs_ref, zeros_ref, out_ref, window, sem):
    del zeros_ref
    size = theirs_ref.shape[1]
    row_base, column_base, down, across = window_of(
        offsets_ref, out_ref.shape[1], out_ref.shape[2], size
    )
    update = jnp.concatenate([ours_ref[...] + theirs_ref[...], jnp.zeros((8, size), F32)], axis=0)
    update = pltpu.roll(pltpu.roll(update, down, 0), lax.rem(across, size), 1)
    lane = lax.broadcasted_iota(jnp.int32, (size + 8, size), 1)
    window[:, :size] = jnp.where(lane < across, 0.0, update)
    window[:, size:] = jnp.where(lane < across, update, 0.0)
    copy = pltpu.make_async_copy(
        window, out_ref.at[0, pl.ds(row_base, size + 8), pl.ds(column_base, 2 * size)], sem
    )
    copy.start()
    copy.wait()


def table_kernel(message_ref, forward_ref, backward_ref, zeros_ref, blank, sem):
    size = message_ref.shape[1]
    blank[...] = jnp.zeros_like(blank)
    copies = [
        pltpu.make_async_copy(blank, zeros_ref.at[0, pl.ds(row, size)], sem.at[k])
        for k, row in enumerate(range(0, zeros_ref.shape[1], size))
    ]
    for copy in copies:
        copy.start()
    rows = lax.broadcasted_iota(jnp.int32, (size, size), 0)
    columns = lax.broadcasted_iota(jnp.int32, (size, size), 1)
    angle = ((rows * columns) % size).astype(F32) * (2.0 * math.pi / size)
    c, s = sincos(angle)
    whole = jnp.concatenate(
        [jnp.concatenate([c, s], axis=1), jnp.concatenate([-s, c], axis=1)], axis=0
    )

    def put(index, real, imag):
        real_turned, imag_turned = real.T, imag.T
        for ref, quarters in (
            (forward_ref, (real, imag, -imag, real)),
            (backward_ref, (real_turned, -imag_turned, imag_turned, real_turned)),
        ):
            for place, quarter in enumerate(quarters):
                r, k = place // 2 * size, place % 2 * size
                high, low = split(quarter)
                ref[index, 0, r : r + size, k : k + size] = high
                ref[index, 1, r : r + size, k : k + size] = low

    for steps in (1, 2, 3):
        h_real, h_imag = sincos(message_ref[size + 1 : size + 2, :] * float(steps))
        real = c * h_real + s * h_imag
        imag = c * h_imag - s * h_real
        put(2 + steps, real * (1.0 / math.sqrt(size)), imag * (1.0 / math.sqrt(size)))
        both = jnp.concatenate([real, imag], axis=1)
        k = jnp.dot(both, whole, precision=lax.Precision.HIGHEST, preferred_element_type=F32)
        put(steps - 1, k[:, :size] * (1.0 / size), k[:, size:] * (1.0 / size))
    for copy in copies:
        copy.wait()


def steps_of(ref, index, size):
    steps = ref[index, size, 0].astype(jnp.int32)
    return jnp.clip(steps, 1, 3) - 1


def position():
    rank = lax.axis_index("slc")
    return rank, rank // CLUSTER


def patch_of(near_ref, far_ref, at, size):
    block, half, crossed = at // CLUSTER, (at // 2) % 2, at % 2 == 1
    entry = 2 * block + half
    steps = jnp.where(crossed, far_ref[entry, size, 0], near_ref[entry, size, 0])
    kind = jnp.clip(steps.astype(jnp.int32), 1, 3) - 1
    cosine, sine = sincos(jnp.where(crossed, far_ref[entry, :size, :], near_ref[entry, :size, :]))
    return kind, cosine, sine


def first_waves(wave_ref, modes):
    if wave_ref.dtype == F32:
        return [wave_ref[m] for m in range(modes)]
    start = (lax.axis_index("slc") % 2) * modes
    return [
        jnp.concatenate(
            [wave_ref[0, start + m].astype(F32), wave_ref[1, start + m].astype(F32)], axis=1
        )
        for m in range(modes)
    ]


def forward_kernel(condition, chunks, last, near_ref, far_ref, table_ref, table_t_ref, wave_ref, *refs):
    del table_t_ref
    *_, out_ref, kept_ref, sum_ref = refs[-5:-2]
    rank, layer = position()

    size = near_ref.shape[2]
    modes = out_ref.shape[0]

    def run():
        waves = first_waves(wave_ref, modes)
        slices = range(CLUSTER * chunks[0], CLUSTER * chunks[1])
        for index in slices:
            at = index ^ rank
            kind, cosine, sine = patch_of(near_ref, far_ref, at, size)
            if last and index == slices[-1]:
                kind = kind + 3
            if index % 2 == 1:
                cosine, sine = cosine.T, sine.T
            high, low = table_ref[kind, 0], table_ref[kind, 1]
            slot = jnp.minimum(at, 2)
            after = []
            for m in range(modes):
                real, imag = waves[m][:, :size], waves[m][:, size:]
                u = jnp.concatenate(
                    [cosine * real - sine * imag, cosine * imag + sine * real], axis=1
                )
                kept_ref[slot, m] = u
                after.append(two_sided(u, high, low, size))
            waves = after
        total = None
        for m in range(modes):
            out_ref[m] = waves[m]
            if last:
                real, imag = waves[m][:, :size], waves[m][:, size:]
                power = real * real + imag * imag
                total = power if total is None else total + power
        if last:
            sum_ref[...] = total

    pl.when(condition(layer))(run)


def backward_kernel(low_end, high_end, last, near_ref, far_ref, table_ref, kept_ref, *refs):
    if last:
        mine_ref, theirs_ref, measured_ref, *refs = refs
    else:
        refs = refs[1:]
    wave_ref, *outs, ours_ref, _, pulled = refs
    rank, layer = position()

    size = near_ref.shape[2]
    modes = wave_ref.shape[0]

    def run():
        waves = [wave_ref[m] for m in range(modes)]
        if last:
            misfit = mine_ref[...] + theirs_ref[...] - measured_ref[0]
            misfit = jnp.concatenate([misfit, misfit], axis=1)
            waves = [wave * misfit for wave in waves]
        slices = range(CLUSTER * low_end, CLUSTER * high_end)
        for index in reversed(slices):
            at = index ^ rank
            kind, cosine, sine = patch_of(near_ref, far_ref, at, size)
            if last and index == slices[-1]:
                kind = kind + 3
            if index % 2 == 1:
                cosine, sine = cosine.T, sine.T
            high, low = table_ref[kind, 0], table_ref[kind, 1]
            after = []
            for m in range(modes):
                mu = two_sided(waves[m], high, low, size)
                pulled[index - slices[0], m] = mu
                real, imag = mu[:, :size], mu[:, size:]
                if index > 0:
                    after.append(
                        jnp.concatenate(
                            [cosine * real + sine * imag, cosine * imag - sine * real], axis=1
                        )
                    )
            waves = after
        for out_ref in outs:
            for m, wave in enumerate(waves):
                out_ref[m] = wave

    def finish():
        place = rank % CLUSTER
        for odd in range(2):
            index = place // 2 * 2 + odd
            slot = index ^ place
            index = index + CLUSTER * (layer - low_end)
            gradient = None
            for m in range(modes):
                mu, u = pulled[index, m], kept_ref[slot, m]
                term = mu[:, size:] * u[:, :size] - mu[:, :size] * u[:, size:]
                gradient = term if gradient is None else gradient + term
            ours_ref[slot] = gradient.T if odd else gradient

    pl.when(layer < high_end)(run)
    pl.when(jnp.logical_and(layer >= low_end, layer < high_end))(finish)


def choose_kernel(ours_ref, own_ref, other_ref):
    own_ref[...] = ours_ref[0]
    other_ref[...] = ours_ref[1]


def joined_kernel(*refs):
    del refs


def after(block, *others):
    return pl.pallas_call(
        joined_kernel,
        in_specs=[ANY] * (1 + len(others)),
        out_specs=ANY,
        out_shape=jax.ShapeDtypeStruct(block.shape, block.dtype),
        input_output_aliases={0: 0},
        compiler_params=pltpu.CompilerParams(vmem_limit_bytes=2**20),
    )(block, *others)


def shaped(*shape, dtype=F32):
    return jax.ShapeDtypeStruct(shape, dtype)


def call(kernel, ins, outs, out_specs=None, scratch=(), flops=0, limit=LIMIT, **more):
    return pl.pallas_call(
        kernel,
        in_specs=ins,
        out_specs=out_specs or [VMEM] * len(outs),
        out_shape=outs,
        scratch_shapes=list(scratch),
        compiler_params=pltpu.CompilerParams(vmem_limit_bytes=limit),
        cost_estimate=pl.CostEstimate(flops=flops, bytes_accessed=1024, transcendentals=0),
        **more,
    )


def local(potential, thickness, propagator_phase, probe, offsets, measured):
    size = probe.shape[2]
    modes = probe.shape[1] // 2
    length = lax.axis_size("slc")
    chunks = length // CLUSTER
    wave = shaped(modes, size, 2 * size)
    kept_shape = shaped(3, modes, size, 2 * size)
    panel = shaped(size, size)
    pair = shaped(2, size, size)
    table = shaped(6, 2, 2 * size, 2 * size, dtype=BF16)
    dma = pltpu.SemaphoreType.DMA
    window = pltpu.VMEM((size + 8, 2 * size), F32)

    def flipped(block, bit):
        return lax.ppermute(block, "slc", [(i, i ^ bit) for i in range(length)])

    (message,) = call(
        extract_kernel,
        [HBM, HBM, HBM, HBM],
        [shaped(size + 8, size)],
        None,
        [
            window,
            pltpu.SMEM((1, 2), jnp.int32),
            pltpu.SMEM((1,), jnp.int32),
            pltpu.VMEM((1, size), F32),
            dma((4,)),
        ],
        limit=63 * 2**20,
    )(offsets, thickness, propagator_phase.reshape(1, size), potential)
    received = flipped(message, 2)
    forward_table, backward_table, zeros = call(
        table_kernel,
        [VMEM],
        [table, table, shaped(*potential.shape)],
        [VMEM, VMEM, HBM],
        [pltpu.VMEM((size, potential.shape[2]), F32), dma((potential.shape[1] // size,))],
    )(message)
    near = after(jnp.stack([message, received]), forward_table)
    far = flipped(near, 1)
    beside = flipped(near, CLUSTER)
    halves = [flipped(message, CLUSTER * k) for k in range(2, chunks)]
    crossed = [flipped(half, 2) for half in halves]

    def forward(condition, span, near, far, tables, waves, kept, power):
        last = span[1] == chunks
        ins = [near, far, *tables] + ([probe] if span[0] == 0 else [])
        aliases = {}
        if kept is not None:
            aliases = {len(ins) + k: k for k in range(3)}
            ins += [waves, kept, power]
        *results, first, second = call(
            functools.partial(forward_kernel, condition, span, last),
            [VMEM] * len(ins),
            [wave, kept_shape, panel, table, table],
            None,
            input_output_aliases=aliases | {2: 3, 3: 4},
        )(*ins)
        return (first, second), *results

    tables = (forward_table, backward_table)
    state = forward(lambda layer: layer == 0, (0, 1), near, far, tables, None, None, None)
    beside = after(beside, state[1])
    early = (jnp.concatenate([near, beside]), jnp.concatenate([far, flipped(beside, 1)]))
    late = [block for half, cross in zip(halves, crossed) for block in (half, after(cross, state[1]))]
    late = jnp.stack(late)
    late_far = flipped(late, 1)
    state = forward(lambda layer: layer == 1, (0, 1), *early, *state)
    state = forward(lambda layer: layer <= 1, (1, 2), *early, *state)
    blocks = jnp.concatenate([early[0], late])
    others = jnp.concatenate([early[1], after(late_far, state[1])])
    state = forward(lambda layer: layer > 1, (0, 2), blocks, others, *state)
    for start in range(2, chunks, 2):
        span = (start, min(start + 2, chunks))
        state = forward(lambda layer: layer >= 0, span, blocks, others, *state)
    tables, waves, kept, power = state
    backward_table = tables[1]
    ours, waves = None, [waves]
    extra = (power, flipped(power, 1), measured)
    spans = [(chunks - 2, chunks)] + [(k, k + 1) for k in reversed(range(chunks - 2))]
    for low_end, high_end in spans:
        last = high_end == chunks
        ins = [blocks, others, backward_table, kept, *(extra if last else (ours,)), *waves]
        outs = [wave] if low_end > 0 else []
        aliases = {2: len(outs) + 1}
        if not last:
            aliases[4] = len(outs)
        if outs:
            aliases[len(ins) - 1] = 0
        *waves, ours, backward_table = call(
            functools.partial(backward_kernel, low_end, high_end, last),
            [VMEM] * len(ins),
            outs + [pair, table],
            None,
            [pltpu.VMEM((CLUSTER * (high_end - low_end), *wave.shape), F32)],
            input_output_aliases=aliases,
        )(*ins)
    own, other = call(choose_kernel, [VMEM], [panel, panel])(ours)
    (gradient,) = call(
        place_kernel,
        [VMEM, VMEM, VMEM, HBM],
        [shaped(*potential.shape)],
        [HBM],
        [window, dma],
        input_output_aliases={3: 0},
    )(offsets, own, flipped(other, 1), zeros)
    return gradient


def solution(mesh):
    placed = (
        P(("grp", "slc"), None, None),
        P(("grp", "slc")),
        P(),
        P("grp", None, None, None),
        P("grp", None),
        P("grp", None, None),
    )
    return jax.shard_map(
        local, mesh=mesh, in_specs=placed, out_specs=P(("grp", "slc"), None, None), check_vma=False
    )
```

```python
import functools
import math

import jax
import jax.numpy as jnp
from jax import lax
from jax.experimental import pallas as pl
from jax.experimental.pallas import tpu as pltpu
from jax.sharding import PartitionSpec as P

F32 = jnp.float32
BF16 = jnp.bfloat16
CLUSTER = 4
LIMIT = 12 * 2**20
VMEM = pl.BlockSpec(memory_space=pltpu.VMEM)
SMEM = pl.BlockSpec(memory_space=pltpu.SMEM)
HBM = pl.BlockSpec(memory_space=pltpu.HBM)
ANY = pl.BlockSpec(memory_space=pl.ANY)


def sincos(x):
    turns = jnp.floor(x * (2.0 / math.pi) + 0.5)
    r = x - turns * 1.5703125
    r = r - turns * 4.837512969970703125e-4
    r = r - turns * 7.549789948768648e-8
    r2 = r * r
    s = r + r * r2 * (-1.6666654611e-1 + r2 * (8.3321608736e-3 + r2 * -1.9515295891e-4))
    c = 1.0 - 0.5 * r2 + r2 * r2 * (
        4.166664568298827e-2 + r2 * (-1.388731625493765e-3 + r2 * 2.443315711809948e-5)
    )
    quadrant = turns.astype(jnp.int32)
    odd = (quadrant & 1) == 1
    sine = jnp.where(odd, c, s)
    cosine = jnp.where(odd, s, c)
    sine = jnp.where((quadrant & 2) == 2, -sine, sine)
    cosine = jnp.where(((quadrant + 1) & 2) == 2, -cosine, cosine)
    return cosine, sine


def split(x):
    high = x.astype(BF16)
    return high, (x - high.astype(F32)).astype(BF16)


def dot(a, b):
    return jnp.dot(a, b, preferred_element_type=F32)


def product(x, high, low):
    x_high, x_low = split(x)
    return dot(x_high, high) + dot(x_low, high) + dot(x_high, low)


def turned(x, size):
    return jnp.concatenate([x[:, :size].T, x[:, size:].T], axis=1)


def two_sided(x, high, low, size):
    return product(turned(product(x, high, low), size), high, low)


def window_of(offsets_ref, rows, columns, size):
    row, column = offsets_ref[0, 0], offsets_ref[0, 1]
    row_base = jnp.minimum(row // 8 * 8, rows - size - 8)
    column_base = jnp.minimum(column // 128 * 128, columns - 2 * size)
    return (
        pl.multiple_of(row_base, 8),
        pl.multiple_of(column_base, 128),
        row - row_base,
        column - column_base,
    )


def extract_kernel(
    offsets_hbm, thickness_hbm, phase_hbm, potential_ref, out_ref, window, offsets_ref, thickness_ref, phase_ref, sems
):
    size = out_ref.shape[1]
    phases = pltpu.make_async_copy(phase_hbm, phase_ref, sems.at[3])
    phases.start()
    corner = pltpu.make_async_copy(offsets_hbm, offsets_ref, sems.at[0])
    steps = pltpu.make_async_copy(thickness_hbm, thickness_ref, sems.at[1])
    corner.start()
    steps.start()
    corner.wait()
    row_base, column_base, down, across = window_of(
        offsets_ref, potential_ref.shape[1], potential_ref.shape[2], size
    )
    copy = pltpu.make_async_copy(
        potential_ref.at[0, pl.ds(row_base, size + 8), pl.ds(column_base, 2 * size)], window, sems.at[2]
    )
    copy.start()
    steps.wait()
    phases.wait()
    row = lax.broadcasted_iota(jnp.int32, (8, size), 0)
    out_ref[size:, :] = jnp.where(row == 1, phase_ref[...], thickness_ref[0].astype(F32))
    copy.wait()
    part = pltpu.roll(window[...], lax.rem(size + 8 - down, size + 8), 0)[:size]
    shift = lax.rem(size - across, size)
    left = pltpu.roll(part[:, :size], shift, 1)
    right = pltpu.roll(part[:, size:], shift, 1)
    lane = lax.broadcasted_iota(jnp.int32, (size, size), 1)
    out_ref[:size, :] = jnp.where(lane < size - across, left, right)


def place_kernel(offsets_ref, ours_ref, theirs_ref, zeros_ref, out_ref, window, sem):
    del zeros_ref
    size = theirs_ref.shape[1]
    row_base, column_base, down, across = window_of(
        offsets_ref, out_ref.shape[1], out_ref.shape[2], size
    )
    update = jnp.concatenate([ours_ref[...] + theirs_ref[...], jnp.zeros((8, size), F32)], axis=0)
    update = pltpu.roll(pltpu.roll(update, down, 0), lax.rem(across, size), 1)
    lane = lax.broadcasted_iota(jnp.int32, (size + 8, size), 1)
    window[:, :size] = jnp.where(lane < across, 0.0, update)
    window[:, size:] = jnp.where(lane < across, update, 0.0)
    copy = pltpu.make_async_copy(
        window, out_ref.at[0, pl.ds(row_base, size + 8), pl.ds(column_base, 2 * size)], sem
    )
    copy.start()
    copy.wait()


def table_kernel(message_ref, forward_ref, backward_ref, zeros_ref, blank, sem):
    size = message_ref.shape[1]
    blank[...] = jnp.zeros_like(blank)
    copies = [
        pltpu.make_async_copy(blank, zeros_ref.at[0, pl.ds(row, size)], sem.at[k])
        for k, row in enumerate(range(0, zeros_ref.shape[1], size))
    ]
    for copy in copies:
        copy.start()
    rows = lax.broadcasted_iota(jnp.int32, (size, size), 0)
    columns = lax.broadcasted_iota(jnp.int32, (size, size), 1)
    angle = ((rows * columns) % size).astype(F32) * (2.0 * math.pi / size)
    c, s = sincos(angle)
    whole = jnp.concatenate(
        [jnp.concatenate([c, s], axis=1), jnp.concatenate([-s, c], axis=1)], axis=0
    )

    def put(index, real, imag):
        real_turned, imag_turned = real.T, imag.T
        for ref, quarters in (
            (forward_ref, (real, imag, -imag, real)),
            (backward_ref, (real_turned, -imag_turned, imag_turned, real_turned)),
        ):
            for place, quarter in enumerate(quarters):
                r, k = place // 2 * size, place % 2 * size
                high, low = split(quarter)
                ref[index, 0, r : r + size, k : k + size] = high
                ref[index, 1, r : r + size, k : k + size] = low

    for steps in (1, 2, 3):
        h_real, h_imag = sincos(message_ref[size + 1 : size + 2, :] * float(steps))
        real = c * h_real + s * h_imag
        imag = c * h_imag - s * h_real
        put(2 + steps, real * (1.0 / math.sqrt(size)), imag * (1.0 / math.sqrt(size)))
        both = jnp.concatenate([real, imag], axis=1)
        k = jnp.dot(both, whole, precision=lax.Precision.HIGHEST, preferred_element_type=F32)
        put(steps - 1, k[:, :size] * (1.0 / size), k[:, size:] * (1.0 / size))
    for copy in copies:
        copy.wait()


def steps_of(ref, index, size):
    steps = ref[index, size, 0].astype(jnp.int32)
    return jnp.clip(steps, 1, 3) - 1


def position():
    rank = lax.axis_index("slc")
    return rank, rank // CLUSTER


def patch_of(near_ref, far_ref, at, size):
    block, half, crossed = at // CLUSTER, (at // 2) % 2, at % 2 == 1
    entry = 2 * block + half
    steps = jnp.where(crossed, far_ref[entry, size, 0], near_ref[entry, size, 0])
    kind = jnp.clip(steps.astype(jnp.int32), 1, 3) - 1
    cosine, sine = sincos(jnp.where(crossed, far_ref[entry, :size, :], near_ref[entry, :size, :]))
    return kind, cosine, sine


def first_waves(wave_ref, modes):
    if wave_ref.dtype == F32:
        return [wave_ref[m] for m in range(modes)]
    start = (lax.axis_index("slc") % 2) * modes
    return [
        jnp.concatenate(
            [wave_ref[0, start + m].astype(F32), wave_ref[1, start + m].astype(F32)], axis=1
        )
        for m in range(modes)
    ]


def forward_kernel(condition, chunks, last, near_ref, far_ref, table_ref, table_t_ref, wave_ref, *refs):
    del table_t_ref
    *_, out_ref, kept_ref, sum_ref = refs[-5:-2]
    rank, layer = position()

    size = near_ref.shape[2]
    modes = out_ref.shape[0]

    def run():
        waves = first_waves(wave_ref, modes)
        slices = range(CLUSTER * chunks[0], CLUSTER * chunks[1])
        for index in slices:
            at = index ^ rank
            kind, cosine, sine = patch_of(near_ref, far_ref, at, size)
            if last and index == slices[-1]:
                kind = kind + 3
            if index % 2 == 1:
                cosine, sine = cosine.T, sine.T
            high, low = table_ref[kind, 0], table_ref[kind, 1]
            slot = jnp.minimum(at, 2)
            after = []
            for m in range(modes):
                real, imag = waves[m][:, :size], waves[m][:, size:]
                u = jnp.concatenate(
                    [cosine * real - sine * imag, cosine * imag + sine * real], axis=1
                )
                kept_ref[slot, m] = u
                after.append(two_sided(u, high, low, size))
            waves = after
        total = None
        for m in range(modes):
            out_ref[m] = waves[m]
            if last:
                real, imag = waves[m][:, :size], waves[m][:, size:]
                power = real * real + imag * imag
                total = power if total is None else total + power
        if last:
            sum_ref[...] = total

    pl.when(condition(layer))(run)


def backward_kernel(low_end, high_end, last, near_ref, far_ref, table_ref, kept_ref, *refs):
    if last:
        mine_ref, theirs_ref, measured_ref, *refs = refs
    else:
        refs = refs[1:]
    wave_ref, *outs, ours_ref, _, pulled = refs
    rank, layer = position()

    size = near_ref.shape[2]
    modes = wave_ref.shape[0]

    def run():
        waves = [wave_ref[m] for m in range(modes)]
        if last:
            misfit = mine_ref[...] + theirs_ref[...] - measured_ref[0]
            misfit = jnp.concatenate([misfit, misfit], axis=1)
            waves = [wave * misfit for wave in waves]
        slices = range(CLUSTER * low_end, CLUSTER * high_end)
        for index in reversed(slices):
            at = index ^ rank
            kind, cosine, sine = patch_of(near_ref, far_ref, at, size)
            if last and index == slices[-1]:
                kind = kind + 3
            if index % 2 == 1:
                cosine, sine = cosine.T, sine.T
            high, low = table_ref[kind, 0], table_ref[kind, 1]
            after = []
            for m in range(modes):
                mu = two_sided(waves[m], high, low, size)
                pulled[index - slices[0], m] = mu
                real, imag = mu[:, :size], mu[:, size:]
                if index > 0:
                    after.append(
                        jnp.concatenate(
                            [cosine * real + sine * imag, cosine * imag - sine * real], axis=1
                        )
                    )
            waves = after
        for out_ref in outs:
            for m, wave in enumerate(waves):
                out_ref[m] = wave

    def finish():
        place = rank % CLUSTER
        for odd in range(2):
            index = place // 2 * 2 + odd
            slot = index ^ place
            index = index + CLUSTER * (layer - low_end)
            gradient = None
            for m in range(modes):
                mu, u = pulled[index, m], kept_ref[slot, m]
                term = mu[:, size:] * u[:, :size] - mu[:, :size] * u[:, size:]
                gradient = term if gradient is None else gradient + term
            ours_ref[slot] = gradient.T if odd else gradient

    pl.when(layer < high_end)(run)
    pl.when(jnp.logical_and(layer >= low_end, layer < high_end))(finish)


def choose_kernel(ours_ref, own_ref, other_ref):
    own_ref[...] = ours_ref[0]
    other_ref[...] = ours_ref[1]


def joined_kernel(*refs):
    del refs


def after(block, *others):
    return pl.pallas_call(
        joined_kernel,
        in_specs=[ANY] * (1 + len(others)),
        out_specs=ANY,
        out_shape=jax.ShapeDtypeStruct(block.shape, block.dtype),
        input_output_aliases={0: 0},
        compiler_params=pltpu.CompilerParams(vmem_limit_bytes=2**20),
    )(block, *others)


def shaped(*shape, dtype=F32):
    return jax.ShapeDtypeStruct(shape, dtype)


def call(kernel, ins, outs, out_specs=None, scratch=(), flops=0, limit=LIMIT, **more):
    return pl.pallas_call(
        kernel,
        in_specs=ins,
        out_specs=out_specs or [VMEM] * len(outs),
        out_shape=outs,
        scratch_shapes=list(scratch),
        compiler_params=pltpu.CompilerParams(vmem_limit_bytes=limit),
        cost_estimate=pl.CostEstimate(flops=flops, bytes_accessed=1024, transcendentals=0),
        **more,
    )


def local(potential, thickness, propagator_phase, probe, offsets, measured):
    size = probe.shape[2]
    modes = probe.shape[1] // 2
    length = lax.axis_size("slc")
    chunks = length // CLUSTER
    wave = shaped(modes, size, 2 * size)
    kept_shape = shaped(3, modes, size, 2 * size)
    panel = shaped(size, size)
    pair = shaped(2, size, size)
    table = shaped(6, 2, 2 * size, 2 * size, dtype=BF16)
    dma = pltpu.SemaphoreType.DMA
    window = pltpu.VMEM((size + 8, 2 * size), F32)

    def flipped(block, bit):
        return lax.ppermute(block, "slc", [(i, i ^ bit) for i in range(length)])

    (message,) = call(
        extract_kernel,
        [HBM, HBM, HBM, HBM],
        [shaped(size + 8, size)],
        None,
        [
            window,
            pltpu.SMEM((1, 2), jnp.int32),
            pltpu.SMEM((1,), jnp.int32),
            pltpu.VMEM((1, size), F32),
            dma((4,)),
        ],
        limit=63 * 2**20,
    )(offsets, thickness, propagator_phase.reshape(1, size), potential)
    received = flipped(message, 2)
    forward_table, backward_table, zeros = call(
        table_kernel,
        [VMEM],
        [table, table, shaped(*potential.shape)],
        [VMEM, VMEM, HBM],
        [pltpu.VMEM((size, potential.shape[2]), F32), dma((potential.shape[1] // size,))],
    )(message)
    near = after(jnp.stack([message, received]), forward_table)
    far = flipped(near, 1)
    beside = flipped(near, CLUSTER)
    halves = [flipped(message, CLUSTER * k) for k in range(2, chunks)]
    crossed = [flipped(half, 2) for half in halves]

    def forward(condition, span, near, far, tables, waves, kept, power):
        last = span[1] == chunks
        ins = [near, far, *tables] + ([probe] if span[0] == 0 else [])
        aliases = {}
        if kept is not None:
            aliases = {len(ins) + k: k for k in range(3)}
            ins += [waves, kept, power]
        *results, first, second = call(
            functools.partial(forward_kernel, condition, span, last),
            [VMEM] * len(ins),
            [wave, kept_shape, panel, table, table],
            None,
            input_output_aliases=aliases | {2: 3, 3: 4},
        )(*ins)
        return (first, second), *results

    tables = (forward_table, backward_table)
    state = forward(lambda layer: layer == 0, (0, 1), near, far, tables, None, None, None)
    beside = after(beside, state[1])
    early = (jnp.concatenate([near, beside]), jnp.concatenate([far, flipped(beside, 1)]))
    late = [block for half, cross in zip(halves, crossed) for block in (half, after(cross, state[1]))]
    late = jnp.stack(late)
    late_far = flipped(late, 1)
    state = forward(lambda layer: layer == 1, (0, 1), *early, *state)
    state = forward(lambda layer: layer <= 1, (1, 2), *early, *state)
    blocks = jnp.concatenate([early[0], late])
    others = jnp.concatenate([early[1], after(late_far, state[1])])
    state = forward(lambda layer: layer > 1, (0, 2), blocks, others, *state)
    for start in range(2, chunks, 2):
        span = (start, min(start + 2, chunks))
        state = forward(lambda layer: layer >= 0, span, blocks, others, *state)
    tables, waves, kept, power = state
    backward_table = tables[1]
    ours, waves = None, [waves]
    extra = (power, flipped(power, 1), measured)
    spans = [(chunks - 3, chunks)] + [(k, k + 1) for k in reversed(range(chunks - 3))]
    for low_end, high_end in spans:
        last = high_end == chunks
        ins = [blocks, others, backward_table, kept, *(extra if last else (ours,)), *waves]
        outs = [wave] if low_end > 0 else []
        aliases = {2: len(outs) + 1}
        if not last:
            aliases[4] = len(outs)
        if outs:
            aliases[len(ins) - 1] = 0
        *waves, ours, backward_table = call(
            functools.partial(backward_kernel, low_end, high_end, last),
            [VMEM] * len(ins),
            outs + [pair, table],
            None,
            [pltpu.VMEM((CLUSTER * (high_end - low_end), *wave.shape), F32)],
            input_output_aliases=aliases,
        )(*ins)
    own, other = call(choose_kernel, [VMEM], [panel, panel])(ours)
    (gradient,) = call(
        place_kernel,
        [VMEM, VMEM, VMEM, HBM],
        [shaped(*potential.shape)],
        [HBM],
        [window, dma],
        input_output_aliases={3: 0},
    )(offsets, own, flipped(other, 1), zeros)
    return gradient


def solution(mesh):
    placed = (
        P(("grp", "slc"), None, None),
        P(("grp", "slc")),
        P(),
        P("grp", None, None, None),
        P("grp", None),
        P("grp", None, None),
    )
    return jax.shard_map(
        local, mesh=mesh, in_specs=placed, out_specs=P(("grp", "slc"), None, None), check_vma=False
    )
```

```python
import functools
import math

import jax
import jax.numpy as jnp
from jax import lax
from jax.experimental import pallas as pl
from jax.experimental.pallas import tpu as pltpu
from jax.sharding import PartitionSpec as P

F32 = jnp.float32
BF16 = jnp.bfloat16
CLUSTER = 4
LIMIT = 12 * 2**20
VMEM = pl.BlockSpec(memory_space=pltpu.VMEM)
SMEM = pl.BlockSpec(memory_space=pltpu.SMEM)
HBM = pl.BlockSpec(memory_space=pltpu.HBM)
ANY = pl.BlockSpec(memory_space=pl.ANY)


def sincos(x):
    turns = jnp.floor(x * (2.0 / math.pi) + 0.5)
    r = x - turns * 1.5703125
    r = r - turns * 4.837512969970703125e-4
    r = r - turns * 7.549789948768648e-8
    r2 = r * r
    s = r + r * r2 * (-1.6666654611e-1 + r2 * (8.3321608736e-3 + r2 * -1.9515295891e-4))
    c = 1.0 - 0.5 * r2 + r2 * r2 * (
        4.166664568298827e-2 + r2 * (-1.388731625493765e-3 + r2 * 2.443315711809948e-5)
    )
    quadrant = turns.astype(jnp.int32)
    odd = (quadrant & 1) == 1
    sine = jnp.where(odd, c, s)
    cosine = jnp.where(odd, s, c)
    sine = jnp.where((quadrant & 2) == 2, -sine, sine)
    cosine = jnp.where(((quadrant + 1) & 2) == 2, -cosine, cosine)
    return cosine, sine


def split(x):
    high = x.astype(BF16)
    return high, (x - high.astype(F32)).astype(BF16)


def dot(a, b):
    return jnp.dot(a, b, preferred_element_type=F32)


def product(x, high, low):
    x_high, x_low = split(x)
    return dot(x_high, high) + dot(x_low, high) + dot(x_high, low)


def turned(x, size):
    return jnp.concatenate([x[:, :size].T, x[:, size:].T], axis=1)


def two_sided(x, high, low, size):
    return product(turned(product(x, high, low), size), high, low)


def window_of(offsets_ref, rows, columns, size):
    row, column = offsets_ref[0, 0], offsets_ref[0, 1]
    row_base = jnp.minimum(row // 8 * 8, rows - size - 8)
    column_base = jnp.minimum(column // 128 * 128, columns - 2 * size)
    return (
        pl.multiple_of(row_base, 8),
        pl.multiple_of(column_base, 128),
        row - row_base,
        column - column_base,
    )


def extract_kernel(
    offsets_hbm, thickness_hbm, phase_hbm, potential_ref, out_ref, window, offsets_ref, thickness_ref, phase_ref, sems
):
    size = out_ref.shape[1]
    phases = pltpu.make_async_copy(phase_hbm, phase_ref, sems.at[3])
    phases.start()
    corner = pltpu.make_async_copy(offsets_hbm, offsets_ref, sems.at[0])
    steps = pltpu.make_async_copy(thickness_hbm, thickness_ref, sems.at[1])
    corner.start()
    steps.start()
    corner.wait()
    row_base, column_base, down, across = window_of(
        offsets_ref, potential_ref.shape[1], potential_ref.shape[2], size
    )
    copy = pltpu.make_async_copy(
        potential_ref.at[0, pl.ds(row_base, size + 8), pl.ds(column_base, 2 * size)], window, sems.at[2]
    )
    copy.start()
    steps.wait()
    phases.wait()
    row = lax.broadcasted_iota(jnp.int32, (8, size), 0)
    out_ref[size:, :] = jnp.where(row == 1, phase_ref[...], thickness_ref[0].astype(F32))
    copy.wait()
    part = pltpu.roll(window[...], lax.rem(size + 8 - down, size + 8), 0)[:size]
    shift = lax.rem(size - across, size)
    left = pltpu.roll(part[:, :size], shift, 1)
    right = pltpu.roll(part[:, size:], shift, 1)
    lane = lax.broadcasted_iota(jnp.int32, (size, size), 1)
    out_ref[:size, :] = jnp.where(lane < size - across, left, right)


def place_kernel(offsets_ref, ours_ref, theirs_ref, zeros_ref, out_ref, window, sem):
    del zeros_ref
    size = theirs_ref.shape[1]
    row_base, column_base, down, across = window_of(
        offsets_ref, out_ref.shape[1], out_ref.shape[2], size
    )
    update = jnp.concatenate([ours_ref[...] + theirs_ref[...], jnp.zeros((8, size), F32)], axis=0)
    update = pltpu.roll(pltpu.roll(update, down, 0), lax.rem(across, size), 1)
    lane = lax.broadcasted_iota(jnp.int32, (size + 8, size), 1)
    window[:, :size] = jnp.where(lane < across, 0.0, update)
    window[:, size:] = jnp.where(lane < across, update, 0.0)
    copy = pltpu.make_async_copy(
        window, out_ref.at[0, pl.ds(row_base, size + 8), pl.ds(column_base, 2 * size)], sem
    )
    copy.start()
    copy.wait()


def table_kernel(message_ref, forward_ref, backward_ref, zeros_ref, blank, sem):
    size = message_ref.shape[1]
    blank[...] = jnp.zeros_like(blank)
    copies = [
        pltpu.make_async_copy(blank, zeros_ref.at[0, pl.ds(row, size)], sem.at[k])
        for k, row in enumerate(range(0, zeros_ref.shape[1], size))
    ]
    for copy in copies:
        copy.start()
    rows = lax.broadcasted_iota(jnp.int32, (size, size), 0)
    columns = lax.broadcasted_iota(jnp.int32, (size, size), 1)
    angle = ((rows * columns) % size).astype(F32) * (2.0 * math.pi / size)
    c, s = sincos(angle)
    whole = jnp.concatenate(
        [jnp.concatenate([c, s], axis=1), jnp.concatenate([-s, c], axis=1)], axis=0
    )

    def put(index, real, imag):
        real_turned, imag_turned = real.T, imag.T
        for ref, quarters in (
            (forward_ref, (real, imag, -imag, real)),
            (backward_ref, (real_turned, -imag_turned, imag_turned, real_turned)),
        ):
            for place, quarter in enumerate(quarters):
                r, k = place // 2 * size, place % 2 * size
                high, low = split(quarter)
                ref[index, 0, r : r + size, k : k + size] = high
                ref[index, 1, r : r + size, k : k + size] = low

    for steps in (1, 2, 3):
        h_real, h_imag = sincos(message_ref[size + 1 : size + 2, :] * float(steps))
        real = c * h_real + s * h_imag
        imag = c * h_imag - s * h_real
        put(2 + steps, real * (1.0 / math.sqrt(size)), imag * (1.0 / math.sqrt(size)))
        both = jnp.concatenate([real, imag], axis=1)
        k = jnp.dot(both, whole, precision=lax.Precision.HIGHEST, preferred_element_type=F32)
        put(steps - 1, k[:, :size] * (1.0 / size), k[:, size:] * (1.0 / size))
    for copy in copies:
        copy.wait()


def steps_of(ref, index, size):
    steps = ref[index, size, 0].astype(jnp.int32)
    return jnp.clip(steps, 1, 3) - 1


def position():
    rank = lax.axis_index("slc")
    return rank, rank // CLUSTER


def patch_of(near_ref, far_ref, at, size):
    block, half, crossed = at // CLUSTER, (at // 2) % 2, at % 2 == 1
    entry = 2 * block + half
    steps = jnp.where(crossed, far_ref[entry, size, 0], near_ref[entry, size, 0])
    kind = jnp.clip(steps.astype(jnp.int32), 1, 3) - 1
    cosine, sine = sincos(jnp.where(crossed, far_ref[entry, :size, :], near_ref[entry, :size, :]))
    return kind, cosine, sine


def first_waves(wave_ref, modes):
    if wave_ref.dtype == F32:
        return [wave_ref[m] for m in range(modes)]
    start = (lax.axis_index("slc") % 2) * modes
    return [
        jnp.concatenate(
            [wave_ref[0, start + m].astype(F32), wave_ref[1, start + m].astype(F32)], axis=1
        )
        for m in range(modes)
    ]


def forward_kernel(condition, chunks, last, near_ref, far_ref, table_ref, table_t_ref, wave_ref, *refs):
    del table_t_ref
    *_, out_ref, kept_ref, sum_ref = refs[-5:-2]
    rank, layer = position()

    size = near_ref.shape[2]
    modes = out_ref.shape[0]

    def run():
        waves = first_waves(wave_ref, modes)
        slices = range(CLUSTER * chunks[0], CLUSTER * chunks[1])
        for index in slices:
            at = index ^ rank
            kind, cosine, sine = patch_of(near_ref, far_ref, at, size)
            if last and index == slices[-1]:
                kind = kind + 3
            if index % 2 == 1:
                cosine, sine = cosine.T, sine.T
            high, low = table_ref[kind, 0], table_ref[kind, 1]
            slot = jnp.minimum(at, 2)
            after = []
            for m in range(modes):
                real, imag = waves[m][:, :size], waves[m][:, size:]
                u = jnp.concatenate(
                    [cosine * real - sine * imag, cosine * imag + sine * real], axis=1
                )
                kept_ref[slot, m] = u
                after.append(two_sided(u, high, low, size))
            waves = after
        total = None
        for m in range(modes):
            out_ref[m] = waves[m]
            if last:
                real, imag = waves[m][:, :size], waves[m][:, size:]
                power = real * real + imag * imag
                total = power if total is None else total + power
        if last:
            sum_ref[...] = total

    pl.when(condition(layer))(run)


def backward_kernel(low_end, high_end, last, near_ref, far_ref, table_ref, kept_ref, *refs):
    if last:
        mine_ref, theirs_ref, measured_ref, *refs = refs
    else:
        refs = refs[1:]
    wave_ref, *outs, ours_ref, _, pulled = refs
    rank, layer = position()

    size = near_ref.shape[2]
    modes = wave_ref.shape[0]

    def run():
        waves = [wave_ref[m] for m in range(modes)]
        if last:
            misfit = mine_ref[...] + theirs_ref[...] - measured_ref[0]
            misfit = jnp.concatenate([misfit, misfit], axis=1)
            waves = [wave * misfit for wave in waves]
        slices = range(CLUSTER * low_end, CLUSTER * high_end)
        for index in reversed(slices):
            at = index ^ rank
            kind, cosine, sine = patch_of(near_ref, far_ref, at, size)
            if last and index == slices[-1]:
                kind = kind + 3
            if index % 2 == 1:
                cosine, sine = cosine.T, sine.T
            high, low = table_ref[kind, 0], table_ref[kind, 1]
            after = []
            for m in range(modes):
                mu = two_sided(waves[m], high, low, size)
                pulled[index - slices[0], m] = mu
                real, imag = mu[:, :size], mu[:, size:]
                if index > 0:
                    after.append(
                        jnp.concatenate(
                            [cosine * real + sine * imag, cosine * imag - sine * real], axis=1
                        )
                    )
            waves = after
        for out_ref in outs:
            for m, wave in enumerate(waves):
                out_ref[m] = wave

    def finish():
        place = rank % CLUSTER
        for odd in range(2):
            index = place // 2 * 2 + odd
            slot = index ^ place
            index = index + CLUSTER * (layer - low_end)
            gradient = None
            for m in range(modes):
                mu, u = pulled[index, m], kept_ref[slot, m]
                term = mu[:, size:] * u[:, :size] - mu[:, :size] * u[:, size:]
                gradient = term if gradient is None else gradient + term
            ours_ref[slot] = gradient.T if odd else gradient

    pl.when(layer < high_end)(run)
    pl.when(jnp.logical_and(layer >= low_end, layer < high_end))(finish)


def choose_kernel(ours_ref, own_ref, other_ref):
    own_ref[...] = ours_ref[0]
    other_ref[...] = ours_ref[1]


def joined_kernel(*refs):
    del refs


def after(block, *others):
    return pl.pallas_call(
        joined_kernel,
        in_specs=[ANY] * (1 + len(others)),
        out_specs=ANY,
        out_shape=jax.ShapeDtypeStruct(block.shape, block.dtype),
        input_output_aliases={0: 0},
        compiler_params=pltpu.CompilerParams(vmem_limit_bytes=2**20),
    )(block, *others)


def shaped(*shape, dtype=F32):
    return jax.ShapeDtypeStruct(shape, dtype)


def call(kernel, ins, outs, out_specs=None, scratch=(), flops=0, limit=LIMIT, **more):
    return pl.pallas_call(
        kernel,
        in_specs=ins,
        out_specs=out_specs or [VMEM] * len(outs),
        out_shape=outs,
        scratch_shapes=list(scratch),
        compiler_params=pltpu.CompilerParams(vmem_limit_bytes=limit),
        cost_estimate=pl.CostEstimate(flops=flops, bytes_accessed=1024, transcendentals=0),
        **more,
    )


def local(potential, thickness, propagator_phase, probe, offsets, measured):
    size = probe.shape[2]
    modes = probe.shape[1] // 2
    length = lax.axis_size("slc")
    chunks = length // CLUSTER
    wave = shaped(modes, size, 2 * size)
    kept_shape = shaped(3, modes, size, 2 * size)
    panel = shaped(size, size)
    pair = shaped(2, size, size)
    table = shaped(6, 2, 2 * size, 2 * size, dtype=BF16)
    dma = pltpu.SemaphoreType.DMA
    window = pltpu.VMEM((size + 8, 2 * size), F32)

    def flipped(block, bit):
        return lax.ppermute(block, "slc", [(i, i ^ bit) for i in range(length)])

    (message,) = call(
        extract_kernel,
        [HBM, HBM, HBM, HBM],
        [shaped(size + 8, size)],
        None,
        [
            window,
            pltpu.SMEM((1, 2), jnp.int32),
            pltpu.SMEM((1,), jnp.int32),
            pltpu.VMEM((1, size), F32),
            dma((4,)),
        ],
        limit=63 * 2**20,
    )(offsets, thickness, propagator_phase.reshape(1, size), potential)
    received = flipped(message, 2)
    forward_table, backward_table, zeros = call(
        table_kernel,
        [VMEM],
        [table, table, shaped(*potential.shape)],
        [VMEM, VMEM, HBM],
        [pltpu.VMEM((size, potential.shape[2]), F32), dma((potential.shape[1] // size,))],
    )(message)
    near = after(jnp.stack([message, received]), forward_table)
    far = flipped(near, 1)
    beside = flipped(near, CLUSTER)
    halves = [flipped(message, CLUSTER * k) for k in range(2, chunks)]
    crossed = [flipped(half, 2) for half in halves]

    def forward(condition, span, near, far, tables, waves, kept, power):
        last = span[1] == chunks
        ins = [near, far, *tables] + ([probe] if span[0] == 0 else [])
        aliases = {}
        if kept is not None:
            aliases = {len(ins) + k: k for k in range(3)}
            ins += [waves, kept, power]
        *results, first, second = call(
            functools.partial(forward_kernel, condition, span, last),
            [VMEM] * len(ins),
            [wave, kept_shape, panel, table, table],
            None,
            input_output_aliases=aliases | {2: 3, 3: 4},
        )(*ins)
        return (first, second), *results

    tables = (forward_table, backward_table)
    state = forward(lambda layer: layer == 0, (0, 1), near, far, tables, None, None, None)
    beside = after(beside, state[1])
    early = (jnp.concatenate([near, beside]), jnp.concatenate([far, flipped(beside, 1)]))
    late = [block for half, cross in zip(halves, crossed) for block in (half, after(cross, state[1]))]
    late = jnp.stack(late)
    late_far = flipped(late, 1)
    state = forward(lambda layer: layer == 1, (0, 1), *early, *state)
    state = forward(lambda layer: layer <= 1, (1, 2), *early, *state)
    blocks = jnp.concatenate([early[0], late])
    others = jnp.concatenate([early[1], after(late_far, state[1])])
    for span in ((0, 1), (1, 2)):
        state = forward(lambda layer: layer > 1, span, blocks, others, *state)
    for start in range(2, chunks, 2):
        span = (start, min(start + 2, chunks))
        state = forward(lambda layer: layer >= 0, span, blocks, others, *state)
    tables, waves, kept, power = state
    backward_table = tables[1]
    ours, waves = None, [waves]
    extra = (power, flipped(power, 1), measured)
    spans = [(chunks - 3, chunks)] + [(k, k + 1) for k in reversed(range(chunks - 3))]
    for low_end, high_end in spans:
        last = high_end == chunks
        ins = [blocks, others, backward_table, kept, *(extra if last else (ours,)), *waves]
        outs = [wave] if low_end > 0 else []
        aliases = {2: len(outs) + 1}
        if not last:
            aliases[4] = len(outs)
        if outs:
            aliases[len(ins) - 1] = 0
        *waves, ours, backward_table = call(
            functools.partial(backward_kernel, low_end, high_end, last),
            [VMEM] * len(ins),
            outs + [pair, table],
            None,
            [pltpu.VMEM((CLUSTER * (high_end - low_end), *wave.shape), F32)],
            input_output_aliases=aliases,
        )(*ins)
    own, other = call(choose_kernel, [VMEM], [panel, panel])(ours)
    (gradient,) = call(
        place_kernel,
        [VMEM, VMEM, VMEM, HBM],
        [shaped(*potential.shape)],
        [HBM],
        [window, dma],
        input_output_aliases={3: 0},
    )(offsets, own, flipped(other, 1), zeros)
    return gradient


def solution(mesh):
    placed = (
        P(("grp", "slc"), None, None),
        P(("grp", "slc")),
        P(),
        P("grp", None, None, None),
        P("grp", None),
        P("grp", None, None),
    )
    return jax.shard_map(
        local, mesh=mesh, in_specs=placed, out_specs=P(("grp", "slc"), None, None), check_vma=False
    )
```
